256 devices in a mesh: dp: 4 (over z_hi, core), seq: 64 (over x, y, z_lo).
Axes of the slice: x: 4, y: 4, z: 8 (z_hi: 2, z_lo: 4; z = z_hi * 4 + z_lo), core: 2. Of those that a mesh axis runs over, the one named last changes fastest.
Arguments:
- queries: bfloat16 [4, 16384, 768], P('dp', 'seq'), may hold values from -8 to 8
- keys: bfloat16 [4, 16384, 768], P('dp', 'seq'), may hold values from -8 to 8
- values: bfloat16 [4, 16384, 768], P('dp', 'seq'), may hold values from -6 to 6
- out_weight: bfloat16 [768, 768], replicated, may hold values from -0.21875 to 0.21875
- out_cotangent: bfloat16 [4, 16384, 768], P('dp', 'seq'), may hold values from -16 to 16
- offsets: int32 [3, 12], replicated, may hold values from 0 to 7, as said below
Outputs:
- mixed: bfloat16 [4, 16384, 768], P('dp', 'seq')
- query_grad: bfloat16 [4, 16384, 768], P('dp', 'seq')
- key_grad: bfloat16 [4, 16384, 768], P('dp', 'seq')
- value_grad: bfloat16 [4, 16384, 768], P('dp', 'seq')
- weight_grad: bfloat16 [768, 768], P('seq')
The draws below stay inside these ranges and needn't reach their ends.
Inputs may be any that keep to these rules, and one draw needn't show every extreme that they name: offsets[k - 1, h] is below 2^k.
All inputs are finite; a program needn't handle non-finite values.
Results may differ from the reference program's by a relative error of at most 0.025.
Values may be sent and summed in bfloat16 or wider, within the bound.
No kernel may reach another device: no remote copies, remote signals or barrier semaphores. Data moves between devices by JAX's collectives and lax.ppermute only.
A program may use at most 64 MiB of HBM per device.

```python
import math
import jax
import jax.numpy as jnp
from jax import lax

D = 768
HEADS = 12
HEAD_DIM = 64
LEVELS = 3
TOK_DEV = 256
SLIDES = 4
TILES = 16384
N_SEQ = 64


def draw_queries(key, part):
    key = jax.random.fold_in(key, 11)
    bulk_values = 1.4 * jax.random.normal(key, (SLIDES, TILES, D))
    return jnp.clip(bulk_values, -8.0, 8.0).astype(jnp.bfloat16)


def draw_keys(key, part):
    key = jax.random.fold_in(key, 12)
    bulk_values = 1.4 * jax.random.normal(key, (SLIDES, TILES, D))
    return jnp.clip(bulk_values, -8.0, 8.0).astype(jnp.bfloat16)


def draw_offsets(key, part):
    key = jax.random.fold_in(key, 3)
    levels_rows = []
    for level_idx in range(LEVELS):
        period = 2 ** (level_idx + 1)
        shuffled = jax.random.permutation(jax.random.fold_in(key, level_idx), HEADS)
        shifted = jax.random.randint(jax.random.fold_in(key, 10 + level_idx), (), 0, period)
        levels_rows.append((shuffled + shifted) % period)
    return jnp.stack(levels_rows).astype(jnp.int32)


def with_spikes(drawn, own_key, source, target, shards_of, factor):
    def block_of(axis_at):
        return (jnp.arange(drawn.shape[axis_at]) // (drawn.shape[axis_at] // shards_of)).reshape((-1,) + (1,) * (drawn.ndim - 1 - axis_at))

    near = jax.random.permutation(own_key, shards_of)[block_of(target)]
    far = (block_of(target) + shards_of // 2) % shards_of
    return jnp.where((block_of(source) == near) | (block_of(source) == far), factor * drawn, drawn)


def levels(stream_key, shape, shards, low, top_value):
    def one(dim, parts):
        heights = jax.random.uniform(jax.random.fold_in(jax.random.fold_in(stream_key, 6), dim), (parts,), jnp.float32, low / len(shards), top_value / len(shards))
        return jnp.repeat(jnp.exp(heights), shape[dim] // parts).reshape((-1,) + (1,) * (len(shape) - dim - 1))

    loudness = one(*shards[0])
    for cut in shards[1:]:
        loudness = loudness * one(*cut)
    return loudness


def noise(stream_key, shape, deviation, most, cuts=(), kind=jnp.bfloat16):
    entries = deviation * jax.random.normal(stream_key, shape, jnp.float32)
    if cuts:
        entries = entries * levels(stream_key, shape, cuts, -0.22, 0.18)
    return jnp.clip(entries, -most, most).astype(kind)


def noise_with(own_key, shape, scale, limit, pieces, heavy, kind=jnp.bfloat16):
    result = scale * jax.random.normal(own_key, shape, jnp.float32)
    if pieces:
        result = result * levels(own_key, shape, pieces, -0.22, 0.18)
    return jnp.clip(with_spikes(result, jax.random.fold_in(own_key, 3), *heavy), -limit, limit).astype(kind)


def setup_inputs(seed: int = 0) -> dict:
    key_list = jax.random.split(jax.random.key(seed), 7)
    return {
        "queries": draw_queries(jax.random.fold_in(key_list[6], 71), 0),
        "keys": draw_keys(jax.random.fold_in(key_list[6], 71), 0),
        "values": noise(key_list[2], (SLIDES, TILES, D), 1.0, 6.0, ((0, 4), (1, 64))),
        "out_weight": noise(key_list[3], (D, D), D ** -0.5, 0.21875),
        "out_cotangent": noise_with(key_list[4], (SLIDES, TILES, D), 1.0, 16.0, ((0, 4), (1, 64)), (1, 2, 64, 4.0)),
        "offsets": draw_offsets(jax.random.fold_in(key_list[6], 71), 0),
    }


def selectors(offsets):
    return [(jnp.arange(2 ** level_idx, dtype=jnp.int32)[:, None] == offsets[level_idx - 1][None, :]).astype(jnp.float32) for level_idx in range(1, LEVELS + 1)]

def thin_out(source, chosen, rate):
    slides, length, feature = source.shape
    regrouped = source.reshape(slides, length // rate, rate, HEADS, HEAD_DIM).astype(jnp.float32)
    picked = jnp.einsum('sarhd,rh->sahd', regrouped, chosen)
    return picked.astype(jnp.bfloat16).reshape(slides, length // rate, feature)

def fill_in(source, chosen, rate):
    slides, row_count, feature = source.shape
    expanded = source.reshape(slides, row_count, 1, HEADS, HEAD_DIM) * chosen[None, None, :, :, None]
    return expanded.reshape(slides, row_count * rate, feature)

def reference(queries, keys, values, out_weight, out_cotangent, offsets):
    slides, length, feature = queries.shape
    rows_dev = TOK_DEV
    score_scale = 1.0 / math.sqrt(HEAD_DIM)
    chosen = selectors(offsets)
    far_keys = [thin_out(keys, chosen[level_idx], 2 ** (level_idx + 1)) for level_idx in range(LEVELS)]
    far_values = [thin_out(values, chosen[level_idx], 2 ** (level_idx + 1)) for level_idx in range(LEVELS)]
    attended_grad = jnp.dot(out_cotangent.reshape(-1, feature), out_weight, preferred_element_type=jnp.float32)
    attended_grad = attended_grad.astype(jnp.bfloat16).reshape(slides, length, feature)

    def blocks(source):
        return source.reshape(slides, N_SEQ, rows_dev, feature).transpose(1, 0, 2, 3)

    def unblock(source):
        return source.transpose(1, 0, 2, 3).reshape(slides, length, feature)

    def step(totals, inputs):
        key_totals, value_totals = totals
        device_idx, query_block, key_block, value_block, grad_block = inputs
        starts = [device_idx // 2 ** (level_idx + 1) * rows_dev for level_idx in range(LEVELS)]
        key_all = jnp.concatenate([key_block] + [lax.dynamic_slice_in_dim(far_keys[level_idx], starts[level_idx], rows_dev, 1) for level_idx in range(LEVELS)], axis=1)
        value_all = jnp.concatenate([value_block] + [lax.dynamic_slice_in_dim(far_values[level_idx], starts[level_idx], rows_dev, 1) for level_idx in range(LEVELS)], axis=1)
        set_rows = key_all.shape[1]
        query_f = query_block.reshape(slides, rows_dev, HEADS, HEAD_DIM).astype(jnp.float32)
        key_f = key_all.reshape(slides, set_rows, HEADS, HEAD_DIM).astype(jnp.float32)
        value_f = value_all.reshape(slides, set_rows, HEADS, HEAD_DIM).astype(jnp.float32)
        grad_f = grad_block.reshape(slides, rows_dev, HEADS, HEAD_DIM).astype(jnp.float32)
        scores = jnp.einsum('sihd,sjhd->shij', query_f, key_f) * score_scale
        row_max = lax.optimization_barrier(jnp.max(scores, axis=-1, keepdims=True))
        raw_weights = jnp.exp(scores - row_max)
        probs = raw_weights / lax.optimization_barrier(jnp.sum(raw_weights, axis=-1, keepdims=True))
        probs_rounded = lax.optimization_barrier(probs.astype(jnp.bfloat16)).astype(jnp.float32)
        attended = jnp.einsum('shij,sjhd->sihd', probs_rounded, value_f).astype(jnp.bfloat16)
        attended_f = lax.optimization_barrier(attended).astype(jnp.float32)
        prob_grad = jnp.einsum('sihd,sjhd->shij', grad_f, value_f)
        delta = lax.optimization_barrier(jnp.sum(grad_f * attended_f, axis=-1)).transpose(0, 2, 1)[..., None]
        score_grad = lax.optimization_barrier((probs * (prob_grad - delta)).astype(jnp.bfloat16)).astype(jnp.float32)
        query_grad = (jnp.einsum('shij,sjhd->sihd', score_grad, key_f) * score_scale).astype(jnp.bfloat16)
        set_key_grad = (jnp.einsum('shij,sihd->sjhd', score_grad, query_f) * score_scale).reshape(slides, set_rows, feature)
        set_value_grad = jnp.einsum('shij,sihd->sjhd', probs_rounded, grad_f).reshape(slides, set_rows, feature)
        new_keys = []
        new_values = []
        for level_idx in range(LEVELS):
            lo_row = (level_idx + 1) * rows_dev
            current = lax.dynamic_slice_in_dim(key_totals[level_idx], starts[level_idx], rows_dev, 1)
            new_keys.append(lax.dynamic_update_slice_in_dim(key_totals[level_idx], current + set_key_grad[:, lo_row:lo_row + rows_dev], starts[level_idx], 1))
            current = lax.dynamic_slice_in_dim(value_totals[level_idx], starts[level_idx], rows_dev, 1)
            new_values.append(lax.dynamic_update_slice_in_dim(value_totals[level_idx], current + set_value_grad[:, lo_row:lo_row + rows_dev], starts[level_idx], 1))
        outputs = (attended.reshape(slides, rows_dev, feature), query_grad.reshape(slides, rows_dev, feature), set_key_grad[:, :rows_dev], set_value_grad[:, :rows_dev])
        return ((tuple(new_keys), tuple(new_values)), outputs)
    initial = tuple((jnp.zeros((slides, length // 2 ** (level_idx + 1), feature), jnp.float32) for level_idx in range(LEVELS)))
    inputs = (jnp.arange(N_SEQ, dtype=jnp.int32), blocks(queries), blocks(keys), blocks(values), blocks(attended_grad))
    (key_totals, value_totals), (attended, query_grad, key_local, value_local) = lax.scan(step, (initial, initial), inputs)
    attended = unblock(attended)
    mixed = jnp.dot(attended.reshape(-1, feature), out_weight.T, preferred_element_type=jnp.float32)
    mixed = mixed.astype(jnp.bfloat16).reshape(slides, length, feature)
    key_grad = unblock(key_local)
    value_grad = unblock(value_local)
    for level_idx in range(LEVELS):
        key_grad = key_grad + fill_in(key_totals[level_idx], chosen[level_idx], 2 ** (level_idx + 1))
        value_grad = value_grad + fill_in(value_totals[level_idx], chosen[level_idx], 2 ** (level_idx + 1))
    weight_grad = jnp.dot(out_cotangent.reshape(-1, feature).T, attended.reshape(-1, feature), preferred_element_type=jnp.float32)
    weight_grad = (weight_grad * (1.0 / math.sqrt(slides * length))).astype(jnp.bfloat16)
    return (mixed, unblock(query_grad), key_grad.astype(jnp.bfloat16), value_grad.astype(jnp.bfloat16), weight_grad)
```

```python
import functools
import math

import jax
import jax.numpy as jnp
from jax import lax
from jax.experimental import pallas as pl
from jax.experimental.pallas import tpu as pltpu
from jax.sharding import PartitionSpec as P

HEADS = 12
HEAD_DIM = 64
LEVELS = 3
PAIR = 2 * HEAD_DIM
VMEM_LIMIT = 48 * 1024 * 1024
F32 = jnp.float32
BF16 = jnp.bfloat16


def lane_masks(row_count):
    lane = lax.broadcasted_iota(jnp.int32, (row_count, PAIR), 1)
    return lane < HEAD_DIM, lane >= HEAD_DIM


def selection(offsets_ref, head, rows_dev, transposed):
    picked_count = rows_dev // 2 + rows_dev // 4 + rows_dev // 8
    shape = (rows_dev, picked_count) if transposed else (picked_count, rows_dev)
    slot = lax.broadcasted_iota(jnp.int32, shape, 1 if transposed else 0)
    row = lax.broadcasted_iota(jnp.int32, shape, 0 if transposed else 1)
    first, second = rows_dev // 2, rows_dev // 2 + rows_dev // 4
    target = jnp.where(
        slot < first,
        2 * slot + offsets_ref[0, head],
        jnp.where(
            slot < second,
            4 * (slot - first) + offsets_ref[1, head],
            8 * (slot - second) + offsets_ref[2, head],
        ),
    )
    return (row == target).astype(F32).astype(BF16)


def pick_kernel(first_pair, offsets_ref, key_ref, value_ref, near_ref, far_ref):
    rows_dev = key_ref.shape[1]
    head = 2 * (first_pair + pl.program_id(0))
    both = jnp.concatenate([key_ref[0], value_ref[0]], axis=1)
    rows = []
    for side in range(2):
        chosen = selection(offsets_ref, head + side, rows_dev, False)
        rows.append(jnp.dot(chosen, both, preferred_element_type=F32))
    low, _ = lane_masks(rows[0].shape[0])
    key_rows = jnp.where(low, rows[0][:, :PAIR], rows[1][:, :PAIR]).astype(BF16)
    value_rows = jnp.where(low, rows[0][:, PAIR:], rows[1][:, PAIR:]).astype(BF16)
    first, second, third = rows_dev // 2, rows_dev // 4, rows_dev // 8
    near_ref[:first] = key_rows[:first]
    near_ref[first:] = value_rows[:first]
    far_ref[:second] = key_rows[first : first + second]
    far_ref[second : 2 * second] = value_rows[first : first + second]
    far_ref[2 * second : 2 * second + third] = key_rows[first + second :]
    far_ref[2 * second + third :] = value_rows[first + second :]


def pick(offsets, keys, values, first_pair, pair_count):
    rows_dev = keys.shape[1]
    width = pair_count * PAIR
    whole = pl.BlockSpec((1, rows_dev, PAIR), lambda i: (0, 0, first_pair + i))
    return pl.pallas_call(
        functools.partial(pick_kernel, first_pair),
        grid=(pair_count,),
        in_specs=[pl.BlockSpec(memory_space=pltpu.SMEM), whole, whole],
        out_specs=[
            pl.BlockSpec((rows_dev, PAIR), lambda i: (0, i)),
            pl.BlockSpec((3 * rows_dev // 4, PAIR), lambda i: (0, i)),
        ],
        out_shape=[
            jax.ShapeDtypeStruct((rows_dev, width), BF16),
            jax.ShapeDtypeStruct((3 * rows_dev // 4, width), BF16),
        ],
        compiler_params=pltpu.CompilerParams(vmem_limit_bytes=VMEM_LIMIT),
        name="pick_rows",
    )(offsets, keys, values)


def attend_kernel(
    query_ref, key_ref, value_ref, grad_ref,
    near_ref, near_pair_ref, far_ref, far_pair_ref,
    third_in_ref, third_out_ref, fourth_in_ref, fourth_out_ref, cross_ref,
    attended_ref, query_grad_ref, local_ref,
    own1_ref, send1_ref, own2_ref, pair2_ref, send2_ref, own3_ref, pair3_ref, send3_ref, cross3_ref,
    keys_scr, values_scr, key_sum, value_sum,
):
    rows_dev = query_ref.shape[1]
    n1, n2, n3 = rows_dev // 2, rows_dev // 4, rows_dev // 8
    keys_scr[:rows_dev] = key_ref[0]
    values_scr[:rows_dev] = value_ref[0]
    at = rows_dev
    for source in (near_ref, near_pair_ref):
        keys_scr[at : at + n1] = source[:n1]
        values_scr[at : at + n1] = source[n1:]
        at += n1
    third = third_in_ref[...] + third_out_ref[...]
    fourth = fourth_in_ref[...] + fourth_out_ref[...]
    blocks = (far_ref[...], far_pair_ref[...], third, fourth)
    for block in blocks:
        keys_scr[at : at + n2] = block[:n2]
        values_scr[at : at + n2] = block[n2 : 2 * n2]
        at += n2
    for block in blocks:
        keys_scr[at : at + n3] = block[2 * n2 : 2 * n2 + n3]
        values_scr[at : at + n3] = block[2 * n2 + n3 :]
        at += n3
    for idx in range(4):
        base = 2 * n3 * idx
        keys_scr[at : at + n3] = cross_ref[base : base + n3]
        values_scr[at : at + n3] = cross_ref[base + n3 : base + 2 * n3]
        at += n3

    query = query_ref[0]
    grad = grad_ref[...]
    scaled = (query.astype(F32) * (1.0 / math.sqrt(HEAD_DIM))).astype(BF16)
    grad_t = grad.T
    keys_t = keys_scr[...].T
    values_t = values_scr[...].T
    nt = (((1,), (1,)), ((), ()))
    attended_parts = []
    query_parts = []
    for side, mask in enumerate(lane_masks(rows_dev)):
        rows = slice(side * HEAD_DIM, (side + 1) * HEAD_DIM)
        query_side = jnp.where(mask, scaled, jnp.zeros_like(scaled))
        grad_side = jnp.where(mask, grad, jnp.zeros_like(grad))
        scores = lax.dot_general(keys_scr[...], query_side, nt, preferred_element_type=F32)
        row_max = jnp.max(scores, axis=0, keepdims=True)
        raw = jnp.exp(scores - row_max)
        probs = raw * (1.0 / jnp.sum(raw, axis=0, keepdims=True))
        rounded = probs.astype(BF16)
        attended = jnp.dot(values_t[rows], rounded, preferred_element_type=F32).astype(BF16)
        attended_parts.append(attended)
        prob_grad = lax.dot_general(values_scr[...], grad_side, nt, preferred_element_type=F32)
        delta = jnp.sum(grad_t[rows].astype(F32) * attended.astype(F32), axis=0, keepdims=True)
        score_grad = (probs * (prob_grad - delta)).astype(BF16)
        query_parts.append(jnp.dot(keys_t[rows], score_grad, preferred_element_type=F32))
        key_part = jnp.dot(score_grad, query_side, preferred_element_type=F32)
        value_part = jnp.dot(rounded, grad_side, preferred_element_type=F32)
        if side == 0:
            key_sum[...] = key_part
            value_sum[...] = value_part
        else:
            key_sum[...] += key_part
            value_sum[...] += value_part
    attended_ref[...] = jnp.concatenate(attended_parts, axis=0).T
    query_t = jnp.concatenate(query_parts, axis=0) * (1.0 / math.sqrt(HEAD_DIM))
    query_grad_ref[0] = query_t.astype(BF16).T

    local_ref[:rows_dev] = key_sum[:rows_dev]
    local_ref[rows_dev:] = value_sum[:rows_dev]
    at = rows_dev
    own1_ref[:n1] = key_sum[at : at + n1]
    own1_ref[n1:] = value_sum[at : at + n1]
    at += n1
    send1_ref[:n1] = key_sum[at : at + n1].astype(BF16)
    send1_ref[n1:] = value_sum[at : at + n1].astype(BF16)
    at += n1
    for refs, step in (((own2_ref, pair2_ref, send2_ref), n2), ((own3_ref, pair3_ref, send3_ref), n3)):
        own, pair, send = refs
        for out, base in ((own, 0), (pair, 0), (send, 0), (send, 2 * step)):
            out[base : base + step] = key_sum[at : at + step].astype(out.dtype)
            out[base + step : base + 2 * step] = value_sum[at : at + step].astype(out.dtype)
            at += step
    for idx in range(4):
        base = 2 * n3 * idx
        cross3_ref[base : base + n3] = key_sum[at : at + n3].astype(BF16)
        cross3_ref[base + n3 : base + 2 * n3] = value_sum[at : at + n3].astype(BF16)
        at += n3


def attend(queries, keys, values, grads, near, near_pair, far, far_pair, third, fourth, cross, first_pair, pair_count):
    rows_dev = queries.shape[1]
    width = pair_count * PAIR
    whole = pl.BlockSpec((1, rows_dev, PAIR), lambda i: (0, 0, first_pair + i))

    def part(count):
        return pl.BlockSpec((count, PAIR), lambda i: (0, i))

    n1, n2, n3 = rows_dev, rows_dev // 2, rows_dev // 4
    far_rows = n2 + n3
    outs = [
        (rows_dev, BF16),
        (None, BF16),
        (2 * rows_dev, F32),
        (n1, F32), (n1, BF16),
        (n2, F32), (n2, F32), (2 * n2, BF16),
        (n3, F32), (n3, F32), (2 * n3, BF16), (4 * n3, BF16),
    ]
    set_rows = 4 * rows_dev
    return pl.pallas_call(
        attend_kernel,
        grid=(pair_count,),
        in_specs=[
            whole, whole, whole,
            pl.BlockSpec((rows_dev, PAIR), lambda i: (0, first_pair + i)),
            part(n1), part(n1),
            part(far_rows), part(far_rows),
            part(far_rows), part(far_rows), part(far_rows), part(far_rows),
            part(4 * n3),
        ],
        out_specs=[
            pl.BlockSpec((1, rows_dev, PAIR), lambda i: (0, 0, i)) if rows is None else part(rows)
            for rows, _ in outs
        ],
        out_shape=[
            jax.ShapeDtypeStruct((1, rows_dev, width) if rows is None else (rows, width), kind)
            for rows, kind in outs
        ],
        scratch_shapes=[
            pltpu.VMEM((set_rows, PAIR), BF16),
            pltpu.VMEM((set_rows, PAIR), BF16),
            pltpu.VMEM((set_rows, PAIR), F32),
            pltpu.VMEM((set_rows, PAIR), F32),
        ],
        compiler_params=pltpu.CompilerParams(vmem_limit_bytes=VMEM_LIMIT),
        cost_estimate=pl.CostEstimate(
            flops=12 * pair_count * 2 * set_rows * rows_dev * HEAD_DIM * 4,
            bytes_accessed=24 * rows_dev * width,
            transcendentals=2 * pair_count * set_rows * rows_dev,
        ),
        name="attend",
    )(queries, keys, values, grads, near, near_pair, far, far_pair, *third, *fourth, cross)


def spread_kernel(
    first_pair, offsets_ref, local_ref, own1_ref, back1_ref,
    own2_ref, mid2_ref, back2_ref, own3_ref, mid3_ref, back3_ref,
    key_ref, value_ref,
):
    rows_dev = local_ref.shape[0] // 2
    head = 2 * (first_pair + pl.program_id(0))
    totals = (
        own1_ref[...] + back1_ref[...].astype(F32),
        own2_ref[...] + mid2_ref[...].astype(F32) + back2_ref[...].astype(F32),
        own3_ref[...] + mid3_ref[...].astype(F32) + back3_ref[...].astype(F32),
    )
    key_rows = jnp.concatenate([t[: t.shape[0] // 2] for t in totals], axis=0)
    value_rows = jnp.concatenate([t[t.shape[0] // 2 :] for t in totals], axis=0)
    both = jnp.concatenate([key_rows, value_rows], axis=1).astype(BF16)
    spread = []
    for side in range(2):
        chosen = selection(offsets_ref, head + side, rows_dev, True)
        spread.append(jnp.dot(chosen, both, preferred_element_type=F32))
    low, _ = lane_masks(rows_dev)
    key_ref[0] = (local_ref[:rows_dev] + jnp.where(low, spread[0][:, :PAIR], spread[1][:, :PAIR])).astype(BF16)
    value_ref[0] = (local_ref[rows_dev:] + jnp.where(low, spread[0][:, PAIR:], spread[1][:, PAIR:])).astype(BF16)


def spread(offsets, parts, first_pair, pair_count):
    rows_dev = parts[0].shape[0] // 2
    width = pair_count * PAIR
    out = pl.BlockSpec((1, rows_dev, PAIR), lambda i: (0, 0, i))
    shape = jax.ShapeDtypeStruct((1, rows_dev, width), BF16)
    return pl.pallas_call(
        functools.partial(spread_kernel, first_pair),
        grid=(pair_count,),
        in_specs=[pl.BlockSpec(memory_space=pltpu.SMEM)]
        + [pl.BlockSpec((part.shape[0], PAIR), lambda i: (0, i)) for part in parts],
        out_specs=[out, out],
        out_shape=[shape, shape],
        compiler_params=pltpu.CompilerParams(vmem_limit_bytes=VMEM_LIMIT),
        name="spread_rows",
    )(offsets, *parts)


def routes(shard_count):
    place = range(shard_count)
    return {
        "pair": [(i, i ^ 1) for i in place],
        "middle": [(i, i + 1 if i % 4 == 1 else i - 1) for i in place if i % 4 in (1, 2)],
        "outward": [(i, i - 1 if i % 4 == 1 else i + 1) for i in place if i % 4 in (1, 2)],
        "inward": [(i, i + 1 if i % 4 == 0 else i - 1) for i in place if i % 4 in (0, 3)],
        "cross": [(i, i ^ 4) for i in place],
    }


def weight_share(cotangent, attended, norm_factor):
    shard_count = lax.axis_size("seq")
    core = lax.axis_index("dp") % 2
    position = lax.axis_index("seq")
    feature = cotangent.shape[1]
    half = feature // 2
    product = lax.dot_general(
        cotangent, attended, (((0,), (0,)), ((), ())), preferred_element_type=F32
    )
    kept = lax.dynamic_slice_in_dim(product, core * half, half, 1)
    sent = lax.dynamic_slice_in_dim(product, (1 - core) * half, half, 1).astype(BF16)
    slide_route = [(i, i ^ 1) for i in range(lax.axis_size("dp"))]
    far_route = [(i, i ^ 2) for i in range(lax.axis_size("dp"))]
    total = (kept + lax.ppermute(sent, "dp", slide_route).astype(F32)).astype(BF16)
    along = 4
    plane = shard_count // along
    x_idx = position // plane
    rows = feature // along
    shares = lax.dynamic_slice_in_dim(total, x_idx * rows, rows, 0).astype(F32)
    for step in (1, 3, 2):
        target = (x_idx + step) % along
        outgoing = lax.dynamic_slice_in_dim(total, target * rows, rows, 0)
        route = [(i, (i + step * plane) % shard_count) for i in range(shard_count)]
        shares = shares + lax.ppermute(outgoing, "seq", route).astype(F32)
    shares = shares.astype(BF16).reshape(plane, rows // plane, half)
    groups = [[g * plane + i for i in range(plane)] for g in range(along)]
    shares = lax.all_to_all(shares, "seq", 0, 0, axis_index_groups=groups, tiled=True)
    shares = jnp.sum(shares.astype(F32), axis=0).astype(BF16)
    other = lax.ppermute(shares, "dp", far_route)
    summed = ((shares.astype(F32) + other.astype(F32)) * norm_factor).astype(BF16)
    across = lax.ppermute(summed, "dp", slide_route)
    return jnp.where(
        core == 0,
        jnp.concatenate([summed, across], 1),
        jnp.concatenate([across, summed], 1),
    )


def gather(near, far, rows_dev, route):
    def move(block, name):
        return lax.ppermute(block, "seq", route[name])

    n3 = rows_dev // 4
    far_pair = move(far, "pair")
    third_in = move(far, "middle")
    fourth_in = move(far_pair, "middle")
    third_out = move(third_in, "outward")
    fourth_out = move(fourth_in, "outward")
    near_pair = move(near, "pair")
    mine = jnp.concatenate(
        [far[-n3:], far_pair[-n3:], (third_in + third_out)[-n3:], (fourth_in + fourth_out)[-n3:]], 0
    )
    cross = move(mine, "cross")
    return near_pair, far_pair, (third_in, third_out), (fourth_in, fourth_out), cross


def give_back(outs, route):
    def move(block, name):
        return lax.ppermute(block, "seq", route[name])

    own1, send1, own2, pair2, send2, own3, pair3, send3, cross3 = outs
    cross = move(cross3, "cross")
    ways = []
    n3 = own3.shape[0]
    own3 = own3 + cross[:n3].astype(F32)
    pair3 = pair3 + cross[n3 : 2 * n3].astype(F32)
    send3 = (send3.astype(F32) + cross[2 * n3 :].astype(F32)).astype(BF16)
    for own, pair, send in ((own2, pair2, send2), (own3, pair3, send3)):
        count = own.shape[0]
        inward = move(send, "inward")
        passed = (send.astype(F32) + inward.astype(F32)).astype(BF16)
        middle = move(passed, "middle")
        last = (pair + middle[count:].astype(F32)).astype(BF16)
        ways.append((own, middle[:count], move(last, "pair")))
    back1 = move(send1, "pair")
    return (own1, back1) + ways[0] + ways[1]


def shards(queries, keys, values, out_weight, out_cotangent, offsets):
    rows_dev, feature = queries.shape[1:]
    cotangent = out_cotangent[0]
    route = routes(lax.axis_size("seq"))
    pairs = HEADS // 2
    near, far = pick(offsets, keys, values, 0, pairs)
    gathered = gather(near, far, rows_dev, route)
    near_pair, far_pair, third, fourth, cross = gathered
    grads = jnp.dot(cotangent, out_weight, preferred_element_type=F32).astype(BF16)
    results = attend(
        queries, keys, values, grads, near, near_pair, far, far_pair, third, fourth, cross, 0, pairs
    )
    attended, query_grad, local = results[:3]
    key_grad, value_grad = spread(offsets, (local,) + give_back(results[3:], route), 0, pairs)
    mixed = lax.dot_general(
        attended, out_weight, (((1,), (1,)), ((), ())), preferred_element_type=F32
    ).astype(BF16)
    tiles = lax.axis_size("dp") * lax.axis_size("seq") * rows_dev
    weight_grad = weight_share(cotangent, attended, 1.0 / math.sqrt(tiles))
    return mixed[None], query_grad, key_grad, value_grad, weight_grad


def solution(mesh):
    split = P("dp", "seq", None)
    return jax.shard_map(
        shards,
        mesh=mesh,
        in_specs=(split, split, split, P(), split, P()),
        out_specs=(split, split, split, split, P("seq", None)),
        check_vma=False,
    )
```

```python
import functools
import math

import jax
import jax.numpy as jnp
from jax import lax
from jax.experimental import pallas as pl
from jax.experimental.pallas import tpu as pltpu
from jax.sharding import PartitionSpec as P

HEADS = 12
HEAD_DIM = 64
LEVELS = 3
PAIR = 2 * HEAD_DIM
VMEM_LIMIT = 60 * 1024 * 1024
LOG2E = 1.0 / math.log(2.0)
GROUPS = ((0, HEADS // 2),)
PICK_PAIRS = 3
SPREAD_PAIRS = 3
CORE_RATE = 10**9
RUN = 4
F32 = jnp.float32
BF16 = jnp.bfloat16


def lane_masks(row_count):
    lane = lax.broadcasted_iota(jnp.int32, (row_count, PAIR), 1)
    return lane < HEAD_DIM, lane >= HEAD_DIM


def selection(offsets_ref, head, rows_dev, transposed):
    picked_count = rows_dev // 2 + rows_dev // 4 + rows_dev // 8
    shape = (rows_dev, picked_count) if transposed else (picked_count, rows_dev)
    slot = lax.broadcasted_iota(jnp.int32, shape, 1 if transposed else 0)
    row = lax.broadcasted_iota(jnp.int32, shape, 0 if transposed else 1)
    first, second = rows_dev // 2, rows_dev // 2 + rows_dev // 4
    target = jnp.where(
        slot < first,
        2 * slot + offsets_ref[0, head],
        jnp.where(
            slot < second,
            4 * (slot - first) + offsets_ref[1, head],
            8 * (slot - second) + offsets_ref[2, head],
        ),
    )
    return (row == target).astype(F32).astype(BF16)


def lanes(pair):
    return slice(pair * PAIR, (pair + 1) * PAIR)


def pick_kernel(offsets_ref, key_ref, value_ref, far_ref, near_ref, mid_ref):
    rows_dev = key_ref.shape[1]
    n1, n2, n3 = rows_dev // 2, rows_dev // 4, rows_dev // 8
    for pair in range(PICK_PAIRS):
        head = 2 * (PICK_PAIRS * pl.program_id(0) + pair)
        at = lanes(pair)
        both = jnp.concatenate([key_ref[0, :, at], value_ref[0, :, at]], axis=1)
        rows = [
            jnp.dot(selection(offsets_ref, head + side, rows_dev, False), both, preferred_element_type=F32)
            for side in range(2)
        ]
        low, _ = lane_masks(rows[0].shape[0])
        key_rows = jnp.where(low, rows[0][:, :PAIR], rows[1][:, :PAIR]).astype(BF16)
        value_rows = jnp.where(low, rows[0][:, PAIR:], rows[1][:, PAIR:]).astype(BF16)
        near_ref[:n1, at] = key_rows[:n1]
        near_ref[n1 : 2 * n1, at] = value_rows[:n1]
        near_ref[2 * n1 : 2 * n1 + n2, at] = key_rows[n1 : n1 + n2]
        near_ref[2 * n1 + n2 :, at] = value_rows[n1 : n1 + n2]
        mid_ref[:n2, at] = key_rows[n1 : n1 + n2]
        mid_ref[n2:, at] = value_rows[n1 : n1 + n2]
        far_ref[:n3, at] = key_rows[n1 + n2 :]
        far_ref[n3:, at] = value_rows[n1 + n2 :]


def pick(offsets, keys, values):
    rows_dev, feature = keys.shape[1:]
    width = PICK_PAIRS * PAIR
    whole = pl.BlockSpec((1, rows_dev, width), lambda i: (0, 0, i))
    rows = (rows_dev // 4, 3 * rows_dev // 2, rows_dev // 2)
    return pl.pallas_call(
        pick_kernel,
        grid=(feature // width,),
        in_specs=[pl.BlockSpec(memory_space=pltpu.SMEM), whole, whole],
        out_specs=[pl.BlockSpec((count, width), lambda i: (0, i)) for count in rows],
        out_shape=[jax.ShapeDtypeStruct((count, feature), BF16) for count in rows],
        compiler_params=pltpu.CompilerParams(vmem_limit_bytes=VMEM_LIMIT),
        cost_estimate=pl.CostEstimate(flops=2 * CORE_RATE, bytes_accessed=2 * 10**6, transcendentals=0),
        name="pick_rows",
    )(offsets, keys, values)


def sides(block):
    return [jnp.where(mask, block, jnp.zeros_like(block)) for mask in lane_masks(block.shape[0])]


def head_rows(side):
    return slice(side * HEAD_DIM, (side + 1) * HEAD_DIM)


NT = (((1,), (1,)), ((), ()))


def fill_sets(key_set_ref, value_set_ref, key_ref, value_ref, near_ref, gathered_refs):
    near_pair_ref, mid2_ref, mid3_ref, far0_ref, far1_ref, far2_ref, far3_ref, cross_ref = gathered_refs
    rows_dev = key_ref.shape[1]
    n1, n2, n3 = rows_dev // 2, rows_dev // 4, rows_dev // 8
    key_set_ref[:rows_dev] = key_ref[0]
    value_set_ref[:rows_dev] = value_ref[0]
    sources = [(near_ref, 0, n1), (near_pair_ref, 0, n1)]
    sources += [(near_ref, 2 * n1, n2), (near_pair_ref, 2 * n1, n2), (mid2_ref, 0, n2), (mid3_ref, 0, n2)]
    sources += [(ref, 0, n3) for ref in (far0_ref, far1_ref, far2_ref, far3_ref)]
    sources += [(cross_ref, 2 * n3 * idx, n3) for idx in range(4)]
    at = rows_dev
    for ref, base, count in sources:
        key_set_ref[at : at + count] = ref[base : base + count]
        value_set_ref[at : at + count] = ref[base + count : base + 2 * count]
        at += count


def weights_of(query_sides, keys):
    scores = [lax.dot_general(keys, side, NT, preferred_element_type=F32) for side in query_sides]
    raw, inverse = [], []
    for block in scores:
        row_max = jnp.max(block, axis=0, keepdims=True)
        weights = jnp.exp2(block * LOG2E - row_max * LOG2E)
        inverse.append(1.0 / jnp.sum(weights, axis=0, keepdims=True))
        raw.append(weights.astype(BF16))
    return raw, inverse


def attended_of(values_t, raw, inverse):
    return [
        (jnp.dot(values_t[head_rows(side)], raw[side], preferred_element_type=F32) * inverse[side]).astype(BF16)
        for side in range(2)
    ]


def backward_of(query_sides, grad, attended_t, keys_t, values, raw, raw_pair, inverse, query_grad_ref, out_refs, sums):
    local_ref, own1_ref, own2_ref, far_ref, back_ref, send1_ref, send2_ref, send3_ref = out_refs
    key_sum, value_sum = sums
    rows_dev = grad.shape[0]
    n1, n2, n3 = rows_dev // 2, rows_dev // 4, rows_dev // 8
    grad_t = grad.T.astype(F32)
    normed_t = jnp.concatenate([grad_t[head_rows(side)] * inverse[side] for side in range(2)], axis=0)
    grad_sides = sides(normed_t.astype(BF16).T)
    score_grads = []
    for side in range(2):
        prob_grad = lax.dot_general(values, grad_sides[side], NT, preferred_element_type=F32)
        delta = inverse[side] * jnp.sum(
            grad_t[head_rows(side)] * attended_t[side].astype(F32), axis=0, keepdims=True
        )
        score_grads.append((raw[side].astype(F32) * (prob_grad - delta)).astype(BF16))
    query_t = jnp.concatenate(
        [jnp.dot(keys_t[head_rows(side)], score_grads[side], preferred_element_type=F32) for side in range(2)],
        axis=0,
    )
    query_grad_ref[0] = (query_t * (1.0 / math.sqrt(HEAD_DIM))).astype(BF16).T
    key_sum[...] = jnp.dot(
        jnp.concatenate(score_grads, axis=1), jnp.concatenate(query_sides, axis=0), preferred_element_type=F32
    )
    value_sum[...] = jnp.dot(raw_pair, jnp.concatenate(grad_sides, axis=0), preferred_element_type=F32)
    targets = [(local_ref, 0, rows_dev), (own1_ref, 0, n1), (send1_ref, 0, n1)]
    targets += [(own2_ref, 0, n2), (send1_ref, 2 * n1, n2), (send2_ref, 0, n2), (send3_ref, 0, n2)]
    targets += [(far_ref, 2 * n3 * idx, n3) for idx in range(4)]
    targets += [(back_ref, 2 * n3 * idx, n3) for idx in range(4)]
    at = 0
    for ref, base, count in targets:
        ref[base : base + count] = key_sum[at : at + count].astype(ref.dtype)
        ref[base + count : base + 2 * count] = value_sum[at : at + count].astype(ref.dtype)
        at += count


def scaled_sides(query_ref):
    return sides((query_ref[0].astype(F32) * (1.0 / math.sqrt(HEAD_DIM))).astype(BF16))


def both_kernel(query_ref, key_ref, value_ref, near_ref, *refs):
    gathered, grad_ref, attended_ref, query_grad_ref = refs[:8], refs[8], refs[9], refs[10]
    outs, (key_set, value_set, key_sum, value_sum) = refs[11:-4], refs[-4:]
    fill_sets(key_set, value_set, key_ref, value_ref, near_ref, gathered)
    query_sides = scaled_sides(query_ref)
    raw, inverse = weights_of(query_sides, key_set[...])
    attended_t = attended_of(value_set[...].T, raw, inverse)
    attended_ref[...] = jnp.concatenate(attended_t, axis=0).T
    backward_of(
        query_sides, grad_ref[...], attended_t, key_set[...].T, value_set[...], raw,
        jnp.concatenate(raw, axis=1), inverse, query_grad_ref, outs, (key_sum, value_sum),
    )


class Layout:
    def __init__(self, group, rows_dev, feature):
        self.first, self.count = group
        self.rows_dev, self.feature, self.width = rows_dev, feature, group[1] * PAIR
        self.set_rows = 4 * rows_dev
        self.given = pl.BlockSpec((1, rows_dev, PAIR), lambda i: (0, 0, group[0] + i))
        self.sums = [pltpu.VMEM((self.set_rows, PAIR), F32)] * 2
        self.sets = [pltpu.VMEM((self.set_rows, PAIR), BF16)] * 2

    def whole(self, rows):
        return pl.BlockSpec((rows, PAIR), lambda i: (0, self.first + i))

    def part(self, rows):
        return pl.BlockSpec((rows, PAIR), lambda i: (0, i))

    def of(self, block):
        return self.part(block.shape[0]) if block.shape[1] == self.width else self.whole(block.shape[0])

    def gradient_outs(self):
        rows, shape = self.rows_dev, jax.ShapeDtypeStruct
        wide = [(2 * rows, F32), (rows, F32), (rows // 2, F32), (rows, F32)]
        narrow = [rows, 3 * rows // 2, rows // 2, rows // 2]
        specs = [self.given] + [self.whole(count) for count, _ in wide] + [self.part(count) for count in narrow]
        shapes = [shape((1, rows, self.feature), BF16)]
        shapes += [shape((count, self.feature), kind) for count, kind in wide]
        shapes += [shape((count, self.width), BF16) for count in narrow]
        return specs, shapes

    def call(self, kernel, name, operands, in_specs, out_specs, out_shapes, scratch, micros, before=()):
        return pl.pallas_call(
            kernel,
            grid=(self.count,),
            in_specs=list(in_specs) + [pl.BlockSpec(memory_space=pl.ANY)] * len(before),
            out_specs=out_specs,
            out_shape=out_shapes,
            input_output_aliases={len(operands) + idx: idx for idx in range(len(before))},
            scratch_shapes=scratch,
            compiler_params=pltpu.CompilerParams(vmem_limit_bytes=VMEM_LIMIT),
            cost_estimate=pl.CostEstimate(
                flops=int(micros * self.count * CORE_RATE), bytes_accessed=10**6, transcendentals=0
            ),
            name=name,
        )(*operands, *before)


def attend_both(group, queries, keys, values, grads, near, gathered):
    rows_dev, feature = queries.shape[1:]
    lay = Layout(group, rows_dev, feature)
    specs, shapes = lay.gradient_outs()
    operands = (queries, keys, values, near) + tuple(gathered) + (grads,)
    return lay.call(
        both_kernel, "attend_both", operands, [lay.given] * 3 + [lay.of(block) for block in operands[3:]],
        [lay.whole(rows_dev)] + specs, [jax.ShapeDtypeStruct((rows_dev, feature), BF16)] + shapes,
        lay.sets + lay.sums, 2.6,
    )


def spread_kernel(groups, offsets_ref, local_ref, own1_ref, own2_ref, own3_ref, far1_ref, far2_ref, far3_ref, *refs):
    key_ref, value_ref = refs[-2:]
    rows_dev = local_ref.shape[0] // 2

    def wide(ref, at, rows=slice(None)):
        return ref[rows, at].astype(F32)

    def run(part_refs):
        pair_ref, mid2_ref, mid3_ref = part_refs
        for pair in range(SPREAD_PAIRS):
            head = 2 * (SPREAD_PAIRS * pl.program_id(0) + pair)
            at = lanes(pair)
            totals = (
                own1_ref[:, at] + wide(pair_ref, at, slice(0, rows_dev)),
                own2_ref[:, at] + wide(pair_ref, at, slice(rows_dev, None)) + wide(mid2_ref, at) + wide(mid3_ref, at),
                own3_ref[:, at] + sum(wide(ref, at, slice(0, own3_ref.shape[0])) for ref in (far1_ref, far2_ref, far3_ref)),
            )
            key_rows = jnp.concatenate([t[: t.shape[0] // 2] for t in totals], axis=0)
            value_rows = jnp.concatenate([t[t.shape[0] // 2 :] for t in totals], axis=0)
            both = jnp.concatenate([key_rows, value_rows], axis=1).astype(BF16)
            spread = [
                jnp.dot(selection(offsets_ref, head + side, rows_dev, True), both, preferred_element_type=F32)
                for side in range(2)
            ]
            low, _ = lane_masks(rows_dev)
            key_ref[0, :, at] = (
                local_ref[:rows_dev, at] + jnp.where(low, spread[0][:, :PAIR], spread[1][:, :PAIR])
            ).astype(BF16)
            value_ref[0, :, at] = (
                local_ref[rows_dev:, at] + jnp.where(low, spread[0][:, PAIR:], spread[1][:, PAIR:])
            ).astype(BF16)

    for idx, (first, count) in enumerate(groups):
        step = pl.program_id(0) * SPREAD_PAIRS

        @pl.when((step >= first) & (step < first + count))
        def _():
            run(refs[3 * idx : 3 * idx + 3])


def spread(offsets, local, owns, fars, returned):
    rows_dev, feature = local.shape[0] // 2, local.shape[1]
    width = SPREAD_PAIRS * PAIR
    out = pl.BlockSpec((1, rows_dev, width), lambda i: (0, 0, i))
    shape = jax.ShapeDtypeStruct((1, rows_dev, feature), BF16)
    specs = [pl.BlockSpec((part.shape[0], width), lambda i: (0, i)) for part in (local,) + owns + fars]
    parts = []
    for (first, count), blocks in zip(GROUPS, returned):
        start, last = first // SPREAD_PAIRS, count // SPREAD_PAIRS - 1
        for block in blocks:
            parts.append(block)
            specs.append(
                pl.BlockSpec(
                    (block.shape[0], width),
                    functools.partial(lambda start, last, i: (0, jnp.clip(i - start, 0, last)), start, last),
                )
            )
    return pl.pallas_call(
        functools.partial(spread_kernel, GROUPS),
        grid=(feature // width,),
        in_specs=[pl.BlockSpec(memory_space=pltpu.SMEM)] + specs,
        out_specs=[out, out],
        out_shape=[shape, shape],
        compiler_params=pltpu.CompilerParams(vmem_limit_bytes=VMEM_LIMIT),
        cost_estimate=pl.CostEstimate(flops=3 * CORE_RATE, bytes_accessed=4 * 10**6, transcendentals=0),
        name="spread_rows",
    )(offsets, local, *owns, *fars, *parts)


def swap(block, bits):
    return lax.ppermute(block, "seq", [(i, i ^ bits) for i in range(lax.axis_size("seq"))])


def slide_swap(block, bits):
    return lax.ppermute(block, "dp", [(i, i ^ bits) for i in range(lax.axis_size("dp"))])


def after(block, others):
    tied = lax.optimization_barrier((block,) + tuple(others))
    return tied[0], list(tied[1:])


def plane_share(cotangent, attended):
    core = lax.axis_index("dp") % 2
    half = attended.shape[1] // 2

    def columns(which):
        block = lax.dynamic_slice_in_dim(attended, which * half, half, 1)
        return lax.dot_general(cotangent, block, (((0,), (0,)), ((), ())), preferred_element_type=F32)

    sent = slide_swap(columns(1 - core).astype(BF16), 1)
    total = (columns(core) + sent.astype(F32)).astype(BF16)
    planes = lax.axis_size("seq") // RUN
    groups = [[RUN * place + z for place in range(planes)] for z in range(RUN)]
    shares = lax.all_to_all(total, "seq", 0, 0, axis_index_groups=groups, tiled=True)
    return jnp.sum(shares.reshape(planes, -1, half).astype(F32), axis=0).astype(BF16)


def slides_total(share, norm_factor):
    parts = [slide_swap(share, bits) for bits in (1, 2, 3)]
    mine = ((share.astype(F32) + parts[1].astype(F32)) * norm_factor).astype(BF16)
    other = ((parts[0].astype(F32) + parts[2].astype(F32)) * norm_factor).astype(BF16)
    return jnp.where(
        lax.axis_index("dp") % 2 == 0, jnp.concatenate([mine, other], 1), jnp.concatenate([other, mine], 1)
    )


def shards(queries, keys, values, out_weight, out_cotangent, offsets):
    rows_dev, feature = queries.shape[1:]
    cotangent = out_cotangent[0]
    n3 = rows_dev // 4
    far, near, mid = pick(offsets, keys, values)
    fars = [far] + [swap(far, bits) for bits in (1, 2, 3)]
    cross = swap(jnp.concatenate(fars, axis=0), 4)
    grads = jnp.dot(cotangent, out_weight, preferred_element_type=F32).astype(BF16)
    gathered = [swap(near, 1), swap(mid, 2), swap(mid, 3)] + fars + [cross]
    results = attend_both(GROUPS[0], queries, keys, values, grads, near, gathered)
    attended, query_grad, local, own1, own2, far_grad, back = results[:7]
    cross_back = swap(back, 4)
    back1, back2, back3 = [swap(block, bits) for bits, block in zip((1, 2, 3), results[7:])]
    share = plane_share(cotangent, attended)
    share, (back2, back3) = after(share, [back2, back3])
    far_grad = far_grad + cross_back.astype(F32)
    far_parts = [far_grad[bits * n3 : (bits + 1) * n3] for bits in range(4)]
    rows, half = share.shape[0] // RUN, share.shape[1]
    place = lax.axis_index("seq") % RUN
    share_parts = [lax.dynamic_slice_in_dim(share, (place ^ bits) * rows, rows, 0) for bits in range(4)]
    total = share_parts[0].astype(F32)
    far_back = []
    for bits in (1, 2, 3):
        padded = jnp.pad(share_parts[bits], ((0, -rows % 16), (0, feature - half)))
        arrived = swap(jnp.concatenate([far_parts[bits].astype(BF16), padded], axis=0), bits)
        far_back.append(arrived)
        total = total + arrived[n3 : n3 + rows, :half].astype(F32)
    tiles = lax.axis_size("dp") * lax.axis_size("seq") * rows_dev
    total, (back1,) = after(total.astype(BF16), [back1])
    weight_grad = slides_total(total, 1.0 / math.sqrt(tiles))
    key_grad, value_grad = spread(
        offsets, local, (own1, own2, far_parts[0]), tuple(far_back), [[back1, back2, back3]]
    )
    mixed = lax.dot_general(
        attended, out_weight, (((1,), (1,)), ((), ())), preferred_element_type=F32
    ).astype(BF16)
    return mixed[None], query_grad, key_grad, value_grad, weight_grad


def solution(mesh):
    split = P("dp", "seq", None)
    return jax.shard_map(
        shards,
        mesh=mesh,
        in_specs=(split, split, split, P(), split, P()),
        out_specs=(split, split, split, split, P("seq", None)),
        check_vma=False,
    )
```

```python
import functools
import math

import jax
import jax.numpy as jnp
from jax import lax
from jax.experimental import pallas as pl
from jax.experimental.pallas import tpu as pltpu
from jax.sharding import PartitionSpec as P

HEADS = 12
HEAD_DIM = 64
LEVELS = 3
PAIR = 2 * HEAD_DIM
VMEM_LIMIT = 60 * 1024 * 1024
LOG2E = 1.0 / math.log(2.0)
GROUPS = ((0, HEADS // 2),)
PICK_PAIRS = 3
SPREAD_PAIRS = 3
CORE_RATE = 10**9
RUN = 4
F32 = jnp.float32
BF16 = jnp.bfloat16


def lane_masks(row_count):
    lane = lax.broadcasted_iota(jnp.int32, (row_count, PAIR), 1)
    return lane < HEAD_DIM, lane >= HEAD_DIM


def selection(offsets_ref, head, rows_dev, transposed):
    picked_count = rows_dev // 2 + rows_dev // 4 + rows_dev // 8
    shape = (rows_dev, picked_count) if transposed else (picked_count, rows_dev)
    slot = lax.broadcasted_iota(jnp.int32, shape, 1 if transposed else 0)
    row = lax.broadcasted_iota(jnp.int32, shape, 0 if transposed else 1)
    first, second = rows_dev // 2, rows_dev // 2 + rows_dev // 4
    target = jnp.where(
        slot < first,
        2 * slot + offsets_ref[0, head],
        jnp.where(
            slot < second,
            4 * (slot - first) + offsets_ref[1, head],
            8 * (slot - second) + offsets_ref[2, head],
        ),
    )
    return (row == target).astype(F32).astype(BF16)


def lanes(pair):
    return slice(pair * PAIR, (pair + 1) * PAIR)


def pick_kernel(offsets_ref, key_ref, value_ref, far_ref, near_ref, mid_ref):
    rows_dev = key_ref.shape[1]
    n1, n2, n3 = rows_dev // 2, rows_dev // 4, rows_dev // 8
    for pair in range(PICK_PAIRS):
        head = 2 * (PICK_PAIRS * pl.program_id(0) + pair)
        at = lanes(pair)
        both = jnp.concatenate([key_ref[0, :, at], value_ref[0, :, at]], axis=1)
        rows = [
            jnp.dot(selection(offsets_ref, head + side, rows_dev, False), both, preferred_element_type=F32)
            for side in range(2)
        ]
        low, _ = lane_masks(rows[0].shape[0])
        key_rows = jnp.where(low, rows[0][:, :PAIR], rows[1][:, :PAIR]).astype(BF16)
        value_rows = jnp.where(low, rows[0][:, PAIR:], rows[1][:, PAIR:]).astype(BF16)
        near_ref[:n1, at] = key_rows[:n1]
        near_ref[n1 : 2 * n1, at] = value_rows[:n1]
        near_ref[2 * n1 : 2 * n1 + n2, at] = key_rows[n1 : n1 + n2]
        near_ref[2 * n1 + n2 :, at] = value_rows[n1 : n1 + n2]
        mid_ref[:n2, at] = key_rows[n1 : n1 + n2]
        mid_ref[n2:, at] = value_rows[n1 : n1 + n2]
        far_ref[:n3, at] = key_rows[n1 + n2 :]
        far_ref[n3:, at] = value_rows[n1 + n2 :]


def pick(offsets, keys, values):
    rows_dev, feature = keys.shape[1:]
    width = PICK_PAIRS * PAIR
    whole = pl.BlockSpec((1, rows_dev, width), lambda i: (0, 0, i))
    rows = (rows_dev // 4, 3 * rows_dev // 2, rows_dev // 2)
    return pl.pallas_call(
        pick_kernel,
        grid=(feature // width,),
        in_specs=[pl.BlockSpec(memory_space=pltpu.SMEM), whole, whole],
        out_specs=[pl.BlockSpec((count, width), lambda i: (0, i)) for count in rows],
        out_shape=[jax.ShapeDtypeStruct((count, feature), BF16) for count in rows],
        compiler_params=pltpu.CompilerParams(vmem_limit_bytes=VMEM_LIMIT),
        cost_estimate=pl.CostEstimate(flops=2 * CORE_RATE, bytes_accessed=2 * 10**6, transcendentals=0),
        name="pick_rows",
    )(offsets, keys, values)


def sides(block):
    return [jnp.where(mask, block, jnp.zeros_like(block)) for mask in lane_masks(block.shape[0])]


def head_rows(side):
    return slice(side * HEAD_DIM, (side + 1) * HEAD_DIM)


NT = (((1,), (1,)), ((), ()))


def fill_sets(key_set_ref, value_set_ref, key_ref, value_ref, near_ref, gathered_refs):
    near_pair_ref, mid2_ref, mid3_ref, far0_ref, far1_ref, far2_ref, far3_ref, cross_ref = gathered_refs
    rows_dev = key_ref.shape[1]
    n1, n2, n3 = rows_dev // 2, rows_dev // 4, rows_dev // 8
    key_set_ref[:rows_dev] = key_ref[0]
    value_set_ref[:rows_dev] = value_ref[0]
    sources = [(near_ref, 0, n1), (near_pair_ref, 0, n1)]
    sources += [(near_ref, 2 * n1, n2), (near_pair_ref, 2 * n1, n2), (mid2_ref, 0, n2), (mid3_ref, 0, n2)]
    sources += [(ref, 0, n3) for ref in (far0_ref, far1_ref, far2_ref, far3_ref)]
    sources += [(cross_ref, 2 * n3 * idx, n3) for idx in range(4)]
    at = rows_dev
    for ref, base, count in sources:
        key_set_ref[at : at + count] = ref[base : base + count]
        value_set_ref[at : at + count] = ref[base + count : base + 2 * count]
        at += count


def weights_of(query_sides, keys):
    scores = [lax.dot_general(keys, side, NT, preferred_element_type=F32) for side in query_sides]
    raw, inverse = [], []
    for block in scores:
        row_max = jnp.max(block, axis=0, keepdims=True)
        weights = jnp.exp2(block * LOG2E - row_max * LOG2E)
        inverse.append(1.0 / jnp.sum(weights, axis=0, keepdims=True))
        raw.append(weights.astype(BF16))
    return raw, inverse


def attended_of(values_t, raw, inverse):
    return [
        (jnp.dot(values_t[head_rows(side)], raw[side], preferred_element_type=F32) * inverse[side]).astype(BF16)
        for side in range(2)
    ]


def backward_of(query_sides, grad, attended_t, keys_t, values, raw, raw_pair, inverse, query_grad_ref, out_refs):
    local_ref, own1_ref, own2_ref, far_ref, back_ref, send1_ref, send2_ref, send3_ref = out_refs
    rows_dev = grad.shape[0]
    n1, n2, n3 = rows_dev // 2, rows_dev // 4, rows_dev // 8
    grad_t = grad.T.astype(F32)
    normed_t = jnp.concatenate([grad_t[head_rows(side)] * inverse[side] for side in range(2)], axis=0)
    grad_sides = sides(normed_t.astype(BF16).T)
    score_grads = []
    for side in range(2):
        prob_grad = lax.dot_general(values, grad_sides[side], NT, preferred_element_type=F32)
        delta = inverse[side] * jnp.sum(
            grad_t[head_rows(side)] * attended_t[side].astype(F32), axis=0, keepdims=True
        )
        score_grads.append((raw[side].astype(F32) * (prob_grad - delta)).astype(BF16))
    query_t = jnp.concatenate(
        [jnp.dot(keys_t[head_rows(side)], score_grads[side], preferred_element_type=F32) for side in range(2)],
        axis=0,
    )
    query_grad_ref[0] = (query_t * (1.0 / math.sqrt(HEAD_DIM))).astype(BF16).T
    key_sum = jnp.dot(
        jnp.concatenate(score_grads, axis=1), jnp.concatenate(query_sides, axis=0), preferred_element_type=F32
    )
    value_sum = jnp.dot(raw_pair, jnp.concatenate(grad_sides, axis=0), preferred_element_type=F32)
    targets = [(local_ref, 0, rows_dev), (own1_ref, 0, n1), (send1_ref, 0, n1)]
    targets += [(own2_ref, 0, n2), (send1_ref, 2 * n1, n2), (send2_ref, 0, n2), (send3_ref, 0, n2)]
    targets += [(far_ref, 2 * n3 * idx, n3) for idx in range(4)]
    targets += [(back_ref, 2 * n3 * idx, n3) for idx in range(4)]
    at = 0
    for ref, base, count in targets:
        ref[base : base + count] = key_sum[at : at + count].astype(ref.dtype)
        ref[base + count : base + 2 * count] = value_sum[at : at + count].astype(ref.dtype)
        at += count


def scaled_sides(query_ref):
    return sides((query_ref[0].astype(F32) * (1.0 / math.sqrt(HEAD_DIM))).astype(BF16))


def both_kernel(query_ref, key_ref, value_ref, near_ref, *refs):
    gathered, grad_ref, attended_ref, query_grad_ref = refs[:8], refs[8], refs[9], refs[10]
    outs, (key_set, value_set) = refs[11:-2], refs[-2:]
    fill_sets(key_set, value_set, key_ref, value_ref, near_ref, gathered)
    query_sides = scaled_sides(query_ref)
    raw, inverse = weights_of(query_sides, key_set[...])
    attended_t = attended_of(value_set[...].T, raw, inverse)
    attended_ref[...] = jnp.concatenate(attended_t, axis=0).T
    backward_of(
        query_sides, grad_ref[...], attended_t, key_set[...].T, value_set[...], raw,
        jnp.concatenate(raw, axis=1), inverse, query_grad_ref, outs,
    )


class Layout:
    def __init__(self, group, rows_dev, feature):
        self.first, self.count = group
        self.rows_dev, self.feature, self.width = rows_dev, feature, group[1] * PAIR
        self.set_rows = 4 * rows_dev
        self.given = pl.BlockSpec((1, rows_dev, PAIR), lambda i: (0, 0, group[0] + i))
        self.sets = [pltpu.VMEM((self.set_rows, PAIR), BF16)] * 2

    def whole(self, rows):
        return pl.BlockSpec((rows, PAIR), lambda i: (0, self.first + i))

    def part(self, rows):
        return pl.BlockSpec((rows, PAIR), lambda i: (0, i))

    def of(self, block):
        return self.part(block.shape[0]) if block.shape[1] == self.width else self.whole(block.shape[0])

    def gradient_outs(self):
        rows, shape = self.rows_dev, jax.ShapeDtypeStruct
        wide = [(2 * rows, F32), (rows, F32), (rows // 2, F32), (rows, BF16)]
        narrow = [rows, 3 * rows // 2, rows // 2, rows // 2]
        specs = [self.given] + [self.whole(count) for count, _ in wide] + [self.part(count) for count in narrow]
        shapes = [shape((1, rows, self.feature), BF16)]
        shapes += [shape((count, self.feature), kind) for count, kind in wide]
        shapes += [shape((count, self.width), BF16) for count in narrow]
        return specs, shapes

    def call(self, kernel, name, operands, in_specs, out_specs, out_shapes, scratch, micros, before=()):
        return pl.pallas_call(
            kernel,
            grid=(self.count,),
            in_specs=list(in_specs) + [pl.BlockSpec(memory_space=pl.ANY)] * len(before),
            out_specs=out_specs,
            out_shape=out_shapes,
            input_output_aliases={len(operands) + idx: idx for idx in range(len(before))},
            scratch_shapes=scratch,
            compiler_params=pltpu.CompilerParams(vmem_limit_bytes=VMEM_LIMIT),
            cost_estimate=pl.CostEstimate(
                flops=int(micros * self.count * CORE_RATE), bytes_accessed=10**6, transcendentals=0
            ),
            name=name,
        )(*operands, *before)


def attend_both(group, queries, keys, values, grads, near, gathered):
    rows_dev, feature = queries.shape[1:]
    lay = Layout(group, rows_dev, feature)
    specs, shapes = lay.gradient_outs()
    operands = (queries, keys, values, near) + tuple(gathered) + (grads,)
    return lay.call(
        both_kernel, "attend_both", operands, [lay.given] * 3 + [lay.of(block) for block in operands[3:]],
        [lay.whole(rows_dev)] + specs, [jax.ShapeDtypeStruct((rows_dev, feature), BF16)] + shapes,
        lay.sets, 2.6,
    )


def spread_kernel(groups, offsets_ref, local_ref, own1_ref, own2_ref, own3_ref, far1_ref, far2_ref, far3_ref, *refs):
    key_ref, value_ref = refs[-2:]
    rows_dev = local_ref.shape[0] // 2

    def wide(ref, at, rows=slice(None)):
        return ref[rows, at].astype(F32)

    def run(part_refs):
        pair_ref, mid2_ref, mid3_ref = part_refs
        for pair in range(SPREAD_PAIRS):
            head = 2 * (SPREAD_PAIRS * pl.program_id(0) + pair)
            at = lanes(pair)
            totals = (
                own1_ref[:, at] + wide(pair_ref, at, slice(0, rows_dev)),
                own2_ref[:, at] + wide(pair_ref, at, slice(rows_dev, None)) + wide(mid2_ref, at) + wide(mid3_ref, at),
                wide(own3_ref, at) + sum(wide(ref, at, slice(0, own3_ref.shape[0])) for ref in (far1_ref, far2_ref, far3_ref)),
            )
            key_rows = jnp.concatenate([t[: t.shape[0] // 2] for t in totals], axis=0)
            value_rows = jnp.concatenate([t[t.shape[0] // 2 :] for t in totals], axis=0)
            both = jnp.concatenate([key_rows, value_rows], axis=1).astype(BF16)
            spread = [
                jnp.dot(selection(offsets_ref, head + side, rows_dev, True), both, preferred_element_type=F32)
                for side in range(2)
            ]
            low, _ = lane_masks(rows_dev)
            key_ref[0, :, at] = (
                local_ref[:rows_dev, at] + jnp.where(low, spread[0][:, :PAIR], spread[1][:, :PAIR])
            ).astype(BF16)
            value_ref[0, :, at] = (
                local_ref[rows_dev:, at] + jnp.where(low, spread[0][:, PAIR:], spread[1][:, PAIR:])
            ).astype(BF16)

    for idx, (first, count) in enumerate(groups):
        step = pl.program_id(0) * SPREAD_PAIRS

        @pl.when((step >= first) & (step < first + count))
        def _():
            run(refs[3 * idx : 3 * idx + 3])


def spread(offsets, local, owns, fars, returned):
    rows_dev, feature = local.shape[0] // 2, local.shape[1]
    width = SPREAD_PAIRS * PAIR
    out = pl.BlockSpec((1, rows_dev, width), lambda i: (0, 0, i))
    shape = jax.ShapeDtypeStruct((1, rows_dev, feature), BF16)
    specs = [pl.BlockSpec((part.shape[0], width), lambda i: (0, i)) for part in (local,) + owns + fars]
    specs[3] = pl.BlockSpec((rows_dev // 4, width), lambda i: (0, i))
    parts = []
    for (first, count), blocks in zip(GROUPS, returned):
        start, last = first // SPREAD_PAIRS, count // SPREAD_PAIRS - 1
        for block in blocks:
            parts.append(block)
            specs.append(
                pl.BlockSpec(
                    (block.shape[0], width),
                    functools.partial(lambda start, last, i: (0, jnp.clip(i - start, 0, last)), start, last),
                )
            )
    return pl.pallas_call(
        functools.partial(spread_kernel, GROUPS),
        grid=(feature // width,),
        in_specs=[pl.BlockSpec(memory_space=pltpu.SMEM)] + specs,
        out_specs=[out, out],
        out_shape=[shape, shape],
        compiler_params=pltpu.CompilerParams(vmem_limit_bytes=VMEM_LIMIT),
        cost_estimate=pl.CostEstimate(flops=3 * CORE_RATE, bytes_accessed=4 * 10**6, transcendentals=0),
        name="spread_rows",
    )(offsets, local, *owns, *fars, *parts)


def swap(block, bits):
    return lax.ppermute(block, "seq", [(i, i ^ bits) for i in range(lax.axis_size("seq"))])


def slide_swap(block, bits):
    return lax.ppermute(block, "dp", [(i, i ^ bits) for i in range(lax.axis_size("dp"))])


def after(block, others):
    tied = lax.optimization_barrier((block,) + tuple(others))
    return tied[0], list(tied[1:])


def plane_share(cotangent, attended):
    core = lax.axis_index("dp") % 2
    half = attended.shape[1] // 2

    def columns(which):
        block = lax.dynamic_slice_in_dim(attended, which * half, half, 1)
        return lax.dot_general(cotangent, block, (((0,), (0,)), ((), ())), preferred_element_type=F32)

    sent = slide_swap(columns(1 - core).astype(BF16), 1)
    total = (columns(core) + sent.astype(F32)).astype(BF16)
    planes = lax.axis_size("seq") // RUN
    groups = [[RUN * place + z for place in range(planes)] for z in range(RUN)]
    shares = lax.all_to_all(total, "seq", 0, 0, axis_index_groups=groups, tiled=True)
    return jnp.sum(shares.reshape(planes, -1, half).astype(F32), axis=0).astype(BF16), sent


def slides_total(share, norm_factor):
    mine = ((share.astype(F32) + slide_swap(share, 2).astype(F32)) * norm_factor).astype(BF16)
    other = slide_swap(mine, 1)
    return jnp.where(
        lax.axis_index("dp") % 2 == 0, jnp.concatenate([mine, other], 1), jnp.concatenate([other, mine], 1)
    )


def shards(queries, keys, values, out_weight, out_cotangent, offsets):
    rows_dev, feature = queries.shape[1:]
    cotangent = out_cotangent[0]
    n3 = rows_dev // 4
    far, near, mid = pick(offsets, keys, values)
    fars = [far] + [swap(far, bits) for bits in (1, 2, 3)]
    cross = swap(jnp.concatenate(fars, axis=0), 4)
    grads = jnp.dot(cotangent, out_weight, preferred_element_type=F32).astype(BF16)
    gathered = [swap(near, 1), swap(mid, 2), swap(mid, 3)] + fars + [cross]
    results = attend_both(GROUPS[0], queries, keys, values, grads, near, gathered)
    attended, query_grad, local, own1, own2, far_grad, back = results[:7]
    cross_back = swap(back, 4)
    back1, back2, back3 = [swap(block, bits) for bits, block in zip((1, 2, 3), results[7:])]
    mixed = lax.dot_general(
        attended, out_weight, (((1,), (1,)), ((), ())), preferred_element_type=F32
    ).astype(BF16)
    share, sent = plane_share(cotangent, attended)
    share, (mixed,) = after(share, [mixed])
    far_grad, (back2, back3) = after(far_grad, [back2, back3])
    far_grad = (far_grad.astype(F32) + cross_back.astype(F32)).astype(BF16)
    far_parts = [far_grad[bits * n3 : (bits + 1) * n3] for bits in range(4)]
    rows, half = share.shape[0] // RUN, share.shape[1]
    place = lax.axis_index("seq") % RUN
    share_parts = [lax.dynamic_slice_in_dim(share, (place ^ bits) * rows, rows, 0) for bits in range(4)]
    total = share_parts[0].astype(F32)
    far_back = []
    for bits in (1, 2, 3):
        padded = jnp.pad(share_parts[bits], ((0, -rows % 16), (0, feature - half)))
        arrived = swap(jnp.concatenate([far_parts[bits], padded], axis=0), bits)
        far_back.append(arrived)
        total = total + arrived[n3 : n3 + rows, :half].astype(F32)
    tiles = lax.axis_size("dp") * lax.axis_size("seq") * rows_dev
    total, (back1,) = after(total.astype(BF16), [back1])
    weight_grad = slides_total(total, 1.0 / math.sqrt(tiles))
    key_grad, value_grad = spread(
        offsets, local, (own1, own2, far_grad), tuple(far_back), [[back1, back2, back3]]
    )
    return mixed[None], query_grad, key_grad, value_grad, weight_grad


def solution(mesh):
    split = P("dp", "seq", None)
    return jax.shard_map(
        shards,
        mesh=mesh,
        in_specs=(split, split, split, P(), split, P()),
        out_specs=(split, split, split, split, P("seq", None)),
        check_vma=False,
    )
```

```python
import functools
import math

import jax
import jax.numpy as jnp
from jax import lax
from jax.experimental import pallas as pl
from jax.experimental.pallas import tpu as pltpu
from jax.sharding import PartitionSpec as P

HEADS = 12
HEAD_DIM = 64
LEVELS = 3
PAIR = 2 * HEAD_DIM
VMEM_LIMIT = 60 * 1024 * 1024
LOG2E = 1.0 / math.log(2.0)
GROUPS = ((0, HEADS // 2),)
PICK_PAIRS = 3
SPREAD_PAIRS = 3
CORE_RATE = 10**9
RUN = 4
F32 = jnp.float32
BF16 = jnp.bfloat16


def lane_masks(row_count):
    lane = lax.broadcasted_iota(jnp.int32, (row_count, PAIR), 1)
    return lane < HEAD_DIM, lane >= HEAD_DIM


def selection(offsets_ref, head, rows_dev, levels, transposed):
    counts = [rows_dev >> (level + 1) for level in levels]
    shape = (rows_dev, sum(counts)) if transposed else (sum(counts), rows_dev)
    slot = lax.broadcasted_iota(jnp.int32, shape, 1 if transposed else 0)
    row = lax.broadcasted_iota(jnp.int32, shape, 0 if transposed else 1)
    target, start = None, 0
    for level, count in zip(levels, counts):
        found = (2 << level) * (slot - start) + offsets_ref[level, head]
        target = found if target is None else jnp.where(slot < start, target, found)
        start += count
    return (row == target).astype(F32).astype(BF16)


def lanes(pair):
    return slice(pair * PAIR, (pair + 1) * PAIR)


def pick_kernel(offsets_ref, key_ref, value_ref, far_ref, near_ref, mid_ref):
    rows_dev = key_ref.shape[1]
    n1, n2, n3 = rows_dev // 2, rows_dev // 4, rows_dev // 8
    for pair in range(PICK_PAIRS):
        head = 2 * (PICK_PAIRS * pl.program_id(0) + pair)
        at = lanes(pair)
        both = jnp.concatenate([key_ref[0, :, at], value_ref[0, :, at]], axis=1)
        rows = [
            jnp.dot(selection(offsets_ref, head + side, rows_dev, (0, 1, 2), False), both, preferred_element_type=F32)
            for side in range(2)
        ]
        low, _ = lane_masks(rows[0].shape[0])
        key_rows = jnp.where(low, rows[0][:, :PAIR], rows[1][:, :PAIR]).astype(BF16)
        value_rows = jnp.where(low, rows[0][:, PAIR:], rows[1][:, PAIR:]).astype(BF16)
        near_ref[:n1, at] = key_rows[:n1]
        near_ref[n1 : 2 * n1, at] = value_rows[:n1]
        near_ref[2 * n1 : 2 * n1 + n2, at] = key_rows[n1 : n1 + n2]
        near_ref[2 * n1 + n2 :, at] = value_rows[n1 : n1 + n2]
        mid_ref[:n2, at] = key_rows[n1 : n1 + n2]
        mid_ref[n2:, at] = value_rows[n1 : n1 + n2]
        far_ref[:n3, at] = key_rows[n1 + n2 :]
        far_ref[n3:, at] = value_rows[n1 + n2 :]


def pick(offsets, keys, values):
    rows_dev, feature = keys.shape[1:]
    width = PICK_PAIRS * PAIR
    whole = pl.BlockSpec((1, rows_dev, width), lambda i: (0, 0, i))
    rows = (rows_dev // 4, 3 * rows_dev // 2, rows_dev // 2)
    return pl.pallas_call(
        pick_kernel,
        grid=(feature // width,),
        in_specs=[pl.BlockSpec(memory_space=pltpu.SMEM), whole, whole],
        out_specs=[pl.BlockSpec((count, width), lambda i: (0, i)) for count in rows],
        out_shape=[jax.ShapeDtypeStruct((count, feature), BF16) for count in rows],
        compiler_params=pltpu.CompilerParams(vmem_limit_bytes=VMEM_LIMIT),
        cost_estimate=pl.CostEstimate(flops=2 * CORE_RATE, bytes_accessed=2 * 10**6, transcendentals=0),
        name="pick_rows",
    )(offsets, keys, values)


def sides(block):
    return [jnp.where(mask, block, jnp.zeros_like(block)) for mask in lane_masks(block.shape[0])]


def head_rows(side):
    return slice(side * HEAD_DIM, (side + 1) * HEAD_DIM)


NT = (((1,), (1,)), ((), ()))


def copy_rows(key_set, value_set, key_ref, value_ref, sources):
    at = 0
    if key_ref is not None:
        at = key_ref.shape[1]
        key_set[:at] = key_ref[0]
        value_set[:at] = value_ref[0]
    for ref, base, count in sources:
        key_set[at : at + count] = ref[base : base + count]
        value_set[at : at + count] = ref[base + count : base + 2 * count]
        at += count


def level_rows(rows_dev):
    return rows_dev // 2, rows_dev // 4, rows_dev // 8


def scaled_sides(query_ref):
    return sides((query_ref[0].astype(F32) * (1.0 / math.sqrt(HEAD_DIM))).astype(BF16))


def scores_of(keys, query_side):
    return lax.dot_general(keys, query_side, NT, preferred_element_type=F32)


def own_kernel(query_ref, key_ref, value_ref, near_ref, mid_ref, far_ref, raw_ref, stats_ref, part_ref, key_set, value_set):
    n1, n2, n3 = level_rows(query_ref.shape[1])
    copy_rows(key_set, value_set, key_ref, value_ref, [(near_ref, 0, n1), (mid_ref, 0, n2), (far_ref, 0, n3)])
    values_t = value_set[...].T
    rows_dev = query_ref.shape[1]
    for side, query_side in enumerate(scaled_sides(query_ref)):
        scores = scores_of(key_set[...], query_side)
        row_max = jnp.max(scores, axis=0, keepdims=True)
        weights = jnp.exp2(scores * LOG2E - row_max * LOG2E)
        raw = weights.astype(BF16)
        raw_ref[0, :, side * rows_dev : (side + 1) * rows_dev] = raw
        total = jnp.sum(weights, axis=0, keepdims=True)
        for place, row in enumerate((row_max, total)):
            first = 16 * side + 8 * place
            stats_ref[0, first : first + 8] = jnp.broadcast_to(row, (8, rows_dev))
        part_ref[0, head_rows(side)] = jnp.dot(values_t[head_rows(side)], raw, preferred_element_type=F32)


def both_kernel(query_ref, key_ref, value_ref, near_ref, *refs):
    (near_pair_ref, mid2_ref, mid3_ref, far0_ref, far1_ref, far2_ref, far3_ref, cross_ref,
     grad_ref, mid_ref, own_raw_ref, stats_ref, part_ref) = refs[:13]
    attended_ref, query_grad_ref = refs[13:15]
    local_ref, own1_ref, own2_ref, far_ref, back_ref, send1_ref, send2_ref, send3_ref = refs[15:-2]
    key_set, value_set = refs[-2:]
    rows_dev = query_ref.shape[1]
    n1, n2, n3 = level_rows(rows_dev)
    own = rows_dev + n1 + n2 + n3
    copy_rows(
        key_set, value_set, key_ref, value_ref,
        [(near_ref, 0, n1), (mid_ref, 0, n2), (far0_ref, 0, n3)]
        + [(near_pair_ref, 0, n1), (near_pair_ref, 2 * n1, n2), (mid2_ref, 0, n2), (mid3_ref, 0, n2)]
        + [(ref, 0, n3) for ref in (far1_ref, far2_ref, far3_ref)]
        + [(cross_ref, 2 * n3 * idx, n3) for idx in range(4)],
    )
    query_sides = scaled_sides(query_ref)
    scores = [scores_of(key_set[own:], side) for side in query_sides]
    far_values_t = value_set[own:].T
    raw, scales, attended_t = [], [], []
    for side in range(2):
        own_max, own_sum = (stats_ref[0, first : first + 1] for first in (16 * side, 16 * side + 8))
        row_max = jnp.maximum(own_max, jnp.max(scores[side], axis=0, keepdims=True))
        weights = jnp.exp2(scores[side] * LOG2E - row_max * LOG2E)
        own_factor = jnp.exp2((own_max - row_max) * LOG2E)
        inverse = 1.0 / (own_sum * own_factor + jnp.sum(weights, axis=0, keepdims=True))
        raw.append(weights.astype(BF16))
        scales.append((inverse * own_factor, inverse))
        rows = head_rows(side)
        product = jnp.dot(far_values_t[rows], raw[side], preferred_element_type=F32)
        attended_t.append(((part_ref[0, rows] * own_factor + product) * inverse).astype(BF16))
    attended_ref[...] = jnp.concatenate(attended_t, axis=0).T

    grad_t = grad_ref[...].T.astype(F32)
    own_raw = own_raw_ref[0]
    raws = [(own_raw[:, side * rows_dev : (side + 1) * rows_dev], raw[side]) for side in range(2)]
    deltas = [
        jnp.sum(grad_t[head_rows(side)] * attended_t[side].astype(F32), axis=0, keepdims=True) for side in range(2)
    ]
    score_grads = [[], []]
    value_sums = []
    for part, values in enumerate((value_set[:own], value_set[own:])):
        normed = [grad_t[head_rows(side)] * scales[side][part] for side in range(2)]
        grad_sides = sides(jnp.concatenate(normed, axis=0).astype(BF16).T)
        for side in range(2):
            prob_grad = scores_of(values, grad_sides[side])
            difference = prob_grad - deltas[side] * scales[side][part]
            score_grads[side].append((raws[side][part].astype(F32) * difference).astype(BF16))
        pair = own_raw if part == 0 else jnp.concatenate(raw, axis=1)
        value_sums.append(jnp.dot(pair, jnp.concatenate(grad_sides, axis=0), preferred_element_type=F32))
    value_sum = jnp.concatenate(value_sums, axis=0)
    score_grads = [jnp.concatenate(parts, axis=0) for parts in score_grads]
    keys_t = key_set[...].T
    query_t = jnp.concatenate(
        [jnp.dot(keys_t[head_rows(side)], score_grads[side], preferred_element_type=F32) for side in range(2)],
        axis=0,
    )
    query_grad_ref[0] = (query_t * (1.0 / math.sqrt(HEAD_DIM))).astype(BF16).T
    key_sum = jnp.dot(
        jnp.concatenate(score_grads, axis=1), jnp.concatenate(query_sides, axis=0), preferred_element_type=F32
    )
    targets = [(local_ref, 0, rows_dev), (own1_ref, 0, n1), (own2_ref, 0, n2), (far_ref, 0, n3)]
    targets += [(send1_ref, 0, n1), (send1_ref, 2 * n1, n2), (send2_ref, 0, n2), (send3_ref, 0, n2)]
    targets += [(far_ref, 2 * n3 * idx, n3) for idx in range(1, 4)]
    targets += [(back_ref, 2 * n3 * idx, n3) for idx in range(4)]
    at = 0
    for ref, base, count in targets:
        ref[base : base + count] = key_sum[at : at + count].astype(ref.dtype)
        ref[base + count : base + 2 * count] = value_sum[at : at + count].astype(ref.dtype)
        at += count


class Layout:
    def __init__(self, group, rows_dev, feature):
        self.first, self.count = group
        self.rows_dev, self.feature, self.width = rows_dev, feature, group[1] * PAIR
        self.set_rows = 4 * rows_dev
        self.given = pl.BlockSpec((1, rows_dev, PAIR), lambda i: (0, 0, group[0] + i))
        self.sets = [pltpu.VMEM((self.set_rows, PAIR), BF16)] * 2

    def whole(self, rows):
        return pl.BlockSpec((rows, PAIR), lambda i: (0, self.first + i))

    def part(self, rows):
        return pl.BlockSpec((rows, PAIR), lambda i: (0, i))

    def stacked(self, block):
        return pl.BlockSpec((1,) + block.shape[1:], lambda i: (i, 0, 0))

    def of(self, block):
        return self.part(block.shape[0]) if block.shape[1] == self.width else self.whole(block.shape[0])

    def gradient_outs(self):
        rows, shape = self.rows_dev, jax.ShapeDtypeStruct
        wide = [(2 * rows, F32), (rows, F32), (rows // 2, F32), (rows, BF16)]
        narrow = [rows, 3 * rows // 2, rows // 2, rows // 2]
        specs = [self.given] + [self.whole(count) for count, _ in wide] + [self.part(count) for count in narrow]
        shapes = [shape((1, rows, self.feature), BF16)]
        shapes += [shape((count, self.feature), kind) for count, kind in wide]
        shapes += [shape((count, self.width), BF16) for count in narrow]
        return specs, shapes

    def call(self, kernel, name, operands, in_specs, out_specs, out_shapes, scratch, micros, before=()):
        return pl.pallas_call(
            kernel,
            grid=(self.count,),
            in_specs=list(in_specs) + [pl.BlockSpec(memory_space=pl.ANY)] * len(before),
            out_specs=out_specs,
            out_shape=out_shapes,
            input_output_aliases={len(operands) + idx: idx for idx in range(len(before))},
            scratch_shapes=scratch,
            compiler_params=pltpu.CompilerParams(vmem_limit_bytes=VMEM_LIMIT),
            cost_estimate=pl.CostEstimate(
                flops=int(micros * self.count * CORE_RATE), bytes_accessed=10**6, transcendentals=0
            ),
            name=name,
        )(*operands, *before)


def attend_own(group, queries, keys, values, near, mid, far):
    rows_dev, feature = queries.shape[1:]
    lay = Layout(group, rows_dev, feature)
    own = rows_dev + sum(level_rows(rows_dev))
    shape = jax.ShapeDtypeStruct
    shapes = [
        shape((lay.count, own, 2 * rows_dev), BF16),
        shape((lay.count, 32, rows_dev), F32),
        shape((lay.count, PAIR, rows_dev), F32),
    ]
    operands = (queries, keys, values, near, mid, far)
    return lay.call(
        own_kernel, "attend_own", operands, [lay.given] * 3 + [lay.of(block) for block in operands[3:]],
        [lay.stacked(out) for out in shapes], shapes, [pltpu.VMEM((own, PAIR), BF16)] * 2, 0.1,
    )


def attend_both(group, queries, keys, values, grads, near, mid, gathered, own_parts):
    rows_dev, feature = queries.shape[1:]
    lay = Layout(group, rows_dev, feature)
    specs, shapes = lay.gradient_outs()
    operands = (queries, keys, values, near) + tuple(gathered) + (grads, mid) + tuple(own_parts)
    return lay.call(
        both_kernel, "attend_both", operands,
        [lay.given] * 3 + [lay.of(block) for block in operands[3:-3]] + [lay.stacked(block) for block in own_parts],
        [lay.whole(rows_dev)] + specs, [jax.ShapeDtypeStruct((rows_dev, feature), BF16)] + shapes,
        lay.sets, 2.6,
    )


def spread_kernel(levels, offsets_ref, key_base_ref, value_base_ref, *refs):
    key_ref, value_ref = refs[-2:]
    rows_dev = key_ref.shape[1]
    for pair in range(SPREAD_PAIRS):
        head = 2 * (SPREAD_PAIRS * pl.program_id(0) + pair)
        at = lanes(pair)
        key_rows, value_rows, used = [], [], 0
        for level, starts in levels:
            count = rows_dev >> (level + 1)
            total = sum(
                ref[start : start + 2 * count, at].astype(F32)
                for ref, start in zip(refs[used : used + len(starts)], starts)
            )
            used += len(starts)
            key_rows.append(total[:count])
            value_rows.append(total[count:])
        both = jnp.concatenate(
            [jnp.concatenate(key_rows, axis=0), jnp.concatenate(value_rows, axis=0)], axis=1
        ).astype(BF16)
        spread = [
            jnp.dot(
                selection(offsets_ref, head + side, rows_dev, [level for level, _ in levels], True),
                both,
                preferred_element_type=F32,
            )
            for side in range(2)
        ]
        low, _ = lane_masks(rows_dev)
        for half, (base_ref, ref) in enumerate(((key_base_ref, key_ref), (value_base_ref, value_ref))):
            columns = slice(half * PAIR, (half + 1) * PAIR)
            ref[0, :, at] = (
                base_ref[0, :, at] + jnp.where(low, spread[0][:, columns], spread[1][:, columns])
            ).astype(ref.dtype)


def spread(offsets, base, levels, kind):
    key_base, value_base = base
    rows_dev, feature = key_base.shape[1:]
    width = SPREAD_PAIRS * PAIR
    blocks = [block for _, parts in levels for block, _ in parts]
    out = pl.BlockSpec((1, rows_dev, width), lambda i: (0, 0, i))
    shape = jax.ShapeDtypeStruct((1, rows_dev, feature), kind)
    return pl.pallas_call(
        functools.partial(spread_kernel, [(level, [start for _, start in parts]) for level, parts in levels]),
        grid=(feature // width,),
        in_specs=[
            pl.BlockSpec(memory_space=pltpu.SMEM),
            pl.BlockSpec((1, rows_dev, width), lambda i: (0, 0, i)),
            pl.BlockSpec((1, rows_dev, width), lambda i: (int(key_base is value_base), 0, i)),
        ]
        + [pl.BlockSpec((block.shape[0], width), lambda i: (0, i)) for block in blocks],
        out_specs=[out, out],
        out_shape=[shape, shape],
        compiler_params=pltpu.CompilerParams(vmem_limit_bytes=VMEM_LIMIT),
        cost_estimate=pl.CostEstimate(flops=2 * CORE_RATE, bytes_accessed=4 * 10**6, transcendentals=0),
        name="spread_rows",
    )(offsets, key_base, value_base, *blocks)


def swap(block, bits):
    return lax.ppermute(block, "seq", [(i, i ^ bits) for i in range(lax.axis_size("seq"))])


def slide_swap(block, bits):
    return lax.ppermute(block, "dp", [(i, i ^ bits) for i in range(lax.axis_size("dp"))])


def after(block, others):
    tied = lax.optimization_barrier((block,) + tuple(others))
    return tied[0], list(tied[1:])


def plane_share(cotangent, attended):
    core = lax.axis_index("dp") % 2
    half = attended.shape[1] // 2

    def columns(which):
        block = lax.dynamic_slice_in_dim(attended, which * half, half, 1)
        return lax.dot_general(cotangent, block, (((0,), (0,)), ((), ())), preferred_element_type=F32)

    sent = slide_swap(columns(1 - core).astype(BF16), 1)
    total = (columns(core) + sent.astype(F32)).astype(BF16)
    planes = lax.axis_size("seq") // RUN
    groups = [[RUN * place + z for place in range(planes)] for z in range(RUN)]
    shares = lax.all_to_all(total, "seq", 0, 0, axis_index_groups=groups, tiled=True)
    return jnp.sum(shares.reshape(planes, -1, half).astype(F32), axis=0).astype(BF16), sent


def slides_total(share, norm_factor, others):
    mine = ((share.astype(F32) + slide_swap(share, 2).astype(F32)) * norm_factor).astype(BF16)
    mine, others = after(mine, others)
    other = slide_swap(mine, 1)
    whole = jnp.where(
        lax.axis_index("dp") % 2 == 0, jnp.concatenate([mine, other], 1), jnp.concatenate([other, mine], 1)
    )
    return whole, others


def shards(queries, keys, values, out_weight, out_cotangent, offsets):
    rows_dev, feature = queries.shape[1:]
    cotangent = out_cotangent[0]
    n3 = rows_dev // 4
    far, near, mid = pick(offsets, keys, values)
    fars = [far] + [swap(far, bits) for bits in (1, 2, 3)]
    cross = swap(jnp.concatenate(fars, axis=0), 4)
    near_pair, mid2, mid3 = swap(near, 1), swap(mid, 2), swap(mid, 3)
    grads = jnp.dot(cotangent, out_weight, preferred_element_type=F32).astype(BF16)
    gathered = [near_pair, mid2, mid3] + fars + [cross]
    own_parts = attend_own(GROUPS[0], queries, keys, values, near, mid, far)
    results = attend_both(GROUPS[0], queries, keys, values, grads, near, mid, gathered, own_parts)
    attended, query_grad, local, own1, own2, far_grad, back = results[:7]
    cross_back = swap(back, 4)
    back1, back2, back3 = [swap(block, bits) for bits, block in zip((1, 2, 3), results[7:])]
    mixed = lax.dot_general(
        attended, out_weight, (((1,), (1,)), ((), ())), preferred_element_type=F32
    ).astype(BF16)
    share, sent = plane_share(cotangent, attended)
    share, (mixed,) = after(share, [mixed])
    far_grad, (back2, back3) = after(far_grad, [back2, back3])
    far_grad = (far_grad.astype(F32) + cross_back.astype(F32)).astype(BF16)
    far_parts = [far_grad[bits * n3 : (bits + 1) * n3] for bits in range(4)]
    rows, half = share.shape[0] // RUN, share.shape[1]
    place = lax.axis_index("seq") % RUN
    share_parts = [lax.dynamic_slice_in_dim(share, (place ^ bits) * rows, rows, 0) for bits in range(4)]
    total = share_parts[0].astype(F32)
    far_back = []
    for bits in (1, 2, 3):
        padded = jnp.pad(share_parts[bits], ((0, -rows % 16), (0, feature - half)))
        arrived = swap(jnp.concatenate([far_parts[bits], padded], axis=0), bits)
        far_back.append(arrived)
        total = total + arrived[n3 : n3 + rows, :half].astype(F32)
    tiles = lax.axis_size("dp") * lax.axis_size("seq") * rows_dev
    local = local.reshape(2, rows_dev, feature)
    base = spread(
        offsets,
        (local, local),
        ((0, ((own1, 0), (back1, 0))), (1, ((own2, 0), (back1, rows_dev), (back2, 0), (back3, 0)))),
        F32,
    )
    total, base = after(total.astype(BF16), base)
    key_grad, value_grad = spread(
        offsets, base, ((2, tuple((block, 0) for block in [far_grad] + far_back)),), BF16
    )
    weight_grad, (key_grad, value_grad) = slides_total(
        total, 1.0 / math.sqrt(tiles), [key_grad, value_grad]
    )
    return mixed[None], query_grad, key_grad, value_grad, weight_grad


def solution(mesh):
    split = P("dp", "seq", None)
    return jax.shard_map(
        shards,
        mesh=mesh,
        in_specs=(split, split, split, P(), split, P()),
        out_specs=(split, split, split, split, P("seq", None)),
        check_vma=False,
    )
```

```python
import functools
import math

import jax
import jax.numpy as jnp
from jax import lax
from jax.experimental import pallas as pl
from jax.experimental.pallas import tpu as pltpu
from jax.sharding import PartitionSpec as P

HEADS = 12
HEAD_DIM = 64
LEVELS = 3
PAIR = 2 * HEAD_DIM
VMEM_LIMIT = 60 * 1024 * 1024
LOG2E = 1.0 / math.log(2.0)
GROUPS = ((0, HEADS // 2),)
PICK_PAIRS = 3
SPREAD_PAIRS = 3
CORE_RATE = 10**9
RUN = 4
F32 = jnp.float32
BF16 = jnp.bfloat16


def lane_masks(row_count):
    lane = lax.broadcasted_iota(jnp.int32, (row_count, PAIR), 1)
    return lane < HEAD_DIM, lane >= HEAD_DIM


def selection(offsets_ref, head, rows_dev, levels, transposed):
    counts = [rows_dev >> (level + 1) for level in levels]
    shape = (rows_dev, sum(counts)) if transposed else (sum(counts), rows_dev)
    slot = lax.broadcasted_iota(jnp.int32, shape, 1 if transposed else 0)
    row = lax.broadcasted_iota(jnp.int32, shape, 0 if transposed else 1)
    target, start = None, 0
    for level, count in zip(levels, counts):
        found = (2 << level) * (slot - start) + offsets_ref[level, head]
        target = found if target is None else jnp.where(slot < start, target, found)
        start += count
    return (row == target).astype(F32).astype(BF16)


def lanes(pair):
    return slice(pair * PAIR, (pair + 1) * PAIR)


def pick_kernel(offsets_ref, key_ref, value_ref, far_ref, near_ref, mid_ref):
    rows_dev = key_ref.shape[1]
    n1, n2, n3 = rows_dev // 2, rows_dev // 4, rows_dev // 8
    for pair in range(PICK_PAIRS):
        head = 2 * (PICK_PAIRS * pl.program_id(0) + pair)
        at = lanes(pair)
        both = jnp.concatenate([key_ref[0, :, at], value_ref[0, :, at]], axis=1)
        rows = [
            jnp.dot(selection(offsets_ref, head + side, rows_dev, (0, 1, 2), False), both, preferred_element_type=F32)
            for side in range(2)
        ]
        low, _ = lane_masks(rows[0].shape[0])
        key_rows = jnp.where(low, rows[0][:, :PAIR], rows[1][:, :PAIR]).astype(BF16)
        value_rows = jnp.where(low, rows[0][:, PAIR:], rows[1][:, PAIR:]).astype(BF16)
        near_ref[:n1, at] = key_rows[:n1]
        near_ref[n1 : 2 * n1, at] = value_rows[:n1]
        near_ref[2 * n1 : 2 * n1 + n2, at] = key_rows[n1 : n1 + n2]
        near_ref[2 * n1 + n2 :, at] = value_rows[n1 : n1 + n2]
        mid_ref[:n2, at] = key_rows[n1 : n1 + n2]
        mid_ref[n2:, at] = value_rows[n1 : n1 + n2]
        far_ref[:n3, at] = key_rows[n1 + n2 :]
        far_ref[n3:, at] = value_rows[n1 + n2 :]


def pick(offsets, keys, values):
    rows_dev, feature = keys.shape[1:]
    width = PICK_PAIRS * PAIR
    whole = pl.BlockSpec((1, rows_dev, width), lambda i: (0, 0, i))
    rows = (rows_dev // 4, 3 * rows_dev // 2, rows_dev // 2)
    return pl.pallas_call(
        pick_kernel,
        grid=(feature // width,),
        in_specs=[pl.BlockSpec(memory_space=pltpu.SMEM), whole, whole],
        out_specs=[pl.BlockSpec((count, width), lambda i: (0, i)) for count in rows],
        out_shape=[jax.ShapeDtypeStruct((count, feature), BF16) for count in rows],
        compiler_params=pltpu.CompilerParams(vmem_limit_bytes=VMEM_LIMIT),
        cost_estimate=pl.CostEstimate(flops=2 * CORE_RATE, bytes_accessed=2 * 10**6, transcendentals=0),
        name="pick_rows",
    )(offsets, keys, values)


def sides(block):
    return [jnp.where(mask, block, jnp.zeros_like(block)) for mask in lane_masks(block.shape[0])]


def head_rows(side):
    return slice(side * HEAD_DIM, (side + 1) * HEAD_DIM)


NT = (((1,), (1,)), ((), ()))


def copy_rows(key_set, value_set, key_ref, value_ref, sources):
    at = 0
    if key_ref is not None:
        at = key_ref.shape[1]
        key_set[:at] = key_ref[0]
        value_set[:at] = value_ref[0]
    for ref, base, count in sources:
        key_set[at : at + count] = ref[base : base + count]
        value_set[at : at + count] = ref[base + count : base + 2 * count]
        at += count


def level_rows(rows_dev):
    return rows_dev // 2, rows_dev // 4, rows_dev // 8


def scaled_sides(query_ref):
    return sides((query_ref[0].astype(F32) * (1.0 / math.sqrt(HEAD_DIM))).astype(BF16))


def scores_of(keys, query_side):
    return lax.dot_general(keys, query_side, NT, preferred_element_type=F32)


def own_kernel(query_ref, key_ref, value_ref, near_ref, mid_ref, far_ref, raw_ref, stats_ref, part_ref, key_set, value_set):
    n1, n2, n3 = level_rows(query_ref.shape[1])
    copy_rows(key_set, value_set, key_ref, value_ref, [(near_ref, 0, n1), (mid_ref, 0, n2), (far_ref, 0, n3)])
    values_t = value_set[...].T
    rows_dev = query_ref.shape[1]
    for side, query_side in enumerate(scaled_sides(query_ref)):
        scores = scores_of(key_set[...], query_side)
        row_max = jnp.max(scores, axis=0, keepdims=True)
        weights = jnp.exp2(scores * LOG2E - row_max * LOG2E)
        raw = weights.astype(BF16)
        raw_ref[0, :, side * rows_dev : (side + 1) * rows_dev] = raw
        total = jnp.sum(weights, axis=0, keepdims=True)
        for place, row in enumerate((row_max, total)):
            first = 16 * side + 8 * place
            stats_ref[0, first : first + 8] = jnp.broadcast_to(row, (8, rows_dev))
        part_ref[0, head_rows(side)] = jnp.dot(values_t[head_rows(side)], raw, preferred_element_type=F32)


def both_kernel(query_ref, key_ref, value_ref, near_ref, *refs):
    (near_pair_ref, mid2_ref, mid3_ref, far0_ref, far1_ref, far2_ref, far3_ref, cross_ref,
     grad_ref, mid_ref, own_raw_ref, stats_ref, part_ref) = refs[:13]
    attended_ref, query_grad_ref = refs[13:15]
    local_ref, own1_ref, own2_ref, far_ref, back_ref, send1_ref, send2_ref, send3_ref = refs[15:-2]
    key_set, value_set = refs[-2:]
    rows_dev = query_ref.shape[1]
    n1, n2, n3 = level_rows(rows_dev)
    own = rows_dev + n1 + n2 + n3
    copy_rows(
        key_set, value_set, key_ref, value_ref,
        [(near_ref, 0, n1), (mid_ref, 0, n2), (far0_ref, 0, n3)]
        + [(near_pair_ref, 0, n1), (near_pair_ref, 2 * n1, n2), (mid2_ref, 0, n2), (mid3_ref, 0, n2)]
        + [(ref, 0, n3) for ref in (far1_ref, far2_ref, far3_ref)]
        + [(cross_ref, 2 * n3 * idx, n3) for idx in range(4)],
    )
    query_sides = scaled_sides(query_ref)
    scores = [scores_of(key_set[own:], side) for side in query_sides]
    far_values_t = value_set[own:].T
    raw, scales, attended_t = [], [], []
    for side in range(2):
        own_max, own_sum = (stats_ref[0, first : first + 1] for first in (16 * side, 16 * side + 8))
        row_max = jnp.maximum(own_max, jnp.max(scores[side], axis=0, keepdims=True))
        weights = jnp.exp2(scores[side] * LOG2E - row_max * LOG2E)
        own_factor = jnp.exp2((own_max - row_max) * LOG2E)
        inverse = 1.0 / (own_sum * own_factor + jnp.sum(weights, axis=0, keepdims=True))
        raw.append(weights.astype(BF16))
        scales.append((inverse * own_factor, inverse))
        rows = head_rows(side)
        product = jnp.dot(far_values_t[rows], raw[side], preferred_element_type=F32)
        attended_t.append(((part_ref[0, rows] * own_factor + product) * inverse).astype(BF16))
    attended_ref[...] = jnp.concatenate(attended_t, axis=0).T

    grad_t = grad_ref[...].T.astype(F32)
    own_raw = own_raw_ref[0]
    raws = [(own_raw[:, side * rows_dev : (side + 1) * rows_dev], raw[side]) for side in range(2)]
    score_grads = [[], []]
    value_sums = []
    for part, values in enumerate((value_set[:own], value_set[own:])):
        normed = [(grad_t[head_rows(side)] * scales[side][part]).astype(BF16) for side in range(2)]
        grad_sides = sides(jnp.concatenate(normed, axis=0).T)
        for side in range(2):
            prob_grad = scores_of(values, grad_sides[side])
            delta = jnp.sum(normed[side].astype(F32) * attended_t[side].astype(F32), axis=0, keepdims=True)
            score_grads[side].append((raws[side][part].astype(F32) * (prob_grad - delta)).astype(BF16))
        pair = own_raw if part == 0 else jnp.concatenate(raw, axis=1)
        value_sums.append(jnp.dot(pair, jnp.concatenate(grad_sides, axis=0), preferred_element_type=F32))
    value_sum = jnp.concatenate(value_sums, axis=0)
    score_grads = [jnp.concatenate(parts, axis=0) for parts in score_grads]
    keys_t = key_set[...].T
    query_t = jnp.concatenate(
        [jnp.dot(keys_t[head_rows(side)], score_grads[side], preferred_element_type=F32) for side in range(2)],
        axis=0,
    )
    query_grad_ref[0] = (query_t * (1.0 / math.sqrt(HEAD_DIM))).astype(BF16).T
    key_sum = jnp.dot(
        jnp.concatenate(score_grads, axis=1), jnp.concatenate(query_sides, axis=0), preferred_element_type=F32
    )
    targets = [(local_ref, 0, rows_dev), (own1_ref, 0, n1), (own2_ref, 0, n2), (far_ref, 0, n3)]
    targets += [(send1_ref, 0, n1), (send1_ref, 2 * n1, n2), (send2_ref, 0, n2), (send3_ref, 0, n2)]
    targets += [(far_ref, 2 * n3 * idx, n3) for idx in range(1, 4)]
    targets += [(back_ref, 2 * n3 * idx, n3) for idx in range(4)]
    at = 0
    for ref, base, count in targets:
        ref[base : base + count] = key_sum[at : at + count].astype(ref.dtype)
        ref[base + count : base + 2 * count] = value_sum[at : at + count].astype(ref.dtype)
        at += count


class Layout:
    def __init__(self, group, rows_dev, feature):
        self.first, self.count = group
        self.rows_dev, self.feature, self.width = rows_dev, feature, group[1] * PAIR
        self.set_rows = 4 * rows_dev
        self.given = pl.BlockSpec((1, rows_dev, PAIR), lambda i: (0, 0, group[0] + i))
        self.sets = [pltpu.VMEM((self.set_rows, PAIR), BF16)] * 2

    def whole(self, rows):
        return pl.BlockSpec((rows, PAIR), lambda i: (0, self.first + i))

    def part(self, rows):
        return pl.BlockSpec((rows, PAIR), lambda i: (0, i))

    def stacked(self, block):
        return pl.BlockSpec((1,) + block.shape[1:], lambda i: (i, 0, 0))

    def of(self, block):
        return self.part(block.shape[0]) if block.shape[1] == self.width else self.whole(block.shape[0])

    def gradient_outs(self):
        rows, shape = self.rows_dev, jax.ShapeDtypeStruct
        wide = [(2 * rows, F32), (rows, F32), (rows // 2, F32), (rows, BF16)]
        narrow = [rows, 3 * rows // 2, rows // 2, rows // 2]
        specs = [self.given] + [self.whole(count) for count, _ in wide] + [self.part(count) for count in narrow]
        shapes = [shape((1, rows, self.feature), BF16)]
        shapes += [shape((count, self.feature), kind) for count, kind in wide]
        shapes += [shape((count, self.width), BF16) for count in narrow]
        return specs, shapes

    def call(self, kernel, name, operands, in_specs, out_specs, out_shapes, scratch, micros, before=()):
        return pl.pallas_call(
            kernel,
            grid=(self.count,),
            in_specs=list(in_specs) + [pl.BlockSpec(memory_space=pl.ANY)] * len(before),
            out_specs=out_specs,
            out_shape=out_shapes,
            input_output_aliases={len(operands) + idx: idx for idx in range(len(before))},
            scratch_shapes=scratch,
            compiler_params=pltpu.CompilerParams(vmem_limit_bytes=VMEM_LIMIT),
            cost_estimate=pl.CostEstimate(
                flops=int(micros * self.count * CORE_RATE), bytes_accessed=10**6, transcendentals=0
            ),
            name=name,
        )(*operands, *before)


def attend_own(group, queries, keys, values, near, mid, far):
    rows_dev, feature = queries.shape[1:]
    lay = Layout(group, rows_dev, feature)
    own = rows_dev + sum(level_rows(rows_dev))
    shape = jax.ShapeDtypeStruct
    shapes = [
        shape((lay.count, own, 2 * rows_dev), BF16),
        shape((lay.count, 32, rows_dev), F32),
        shape((lay.count, PAIR, rows_dev), F32),
    ]
    operands = (queries, keys, values, near, mid, far)
    return lay.call(
        own_kernel, "attend_own", operands, [lay.given] * 3 + [lay.of(block) for block in operands[3:]],
        [lay.stacked(out) for out in shapes], shapes, [pltpu.VMEM((own, PAIR), BF16)] * 2, 0.1,
    )


def attend_both(group, queries, keys, values, grads, near, mid, gathered, own_parts):
    rows_dev, feature = queries.shape[1:]
    lay = Layout(group, rows_dev, feature)
    specs, shapes = lay.gradient_outs()
    operands = (queries, keys, values, near) + tuple(gathered) + (grads, mid) + tuple(own_parts)
    return lay.call(
        both_kernel, "attend_both", operands,
        [lay.given] * 3 + [lay.of(block) for block in operands[3:-3]] + [lay.stacked(block) for block in own_parts],
        [lay.whole(rows_dev)] + specs, [jax.ShapeDtypeStruct((rows_dev, feature), BF16)] + shapes,
        lay.sets, 2.6,
    )


def spread_kernel(levels, offsets_ref, key_base_ref, value_base_ref, *refs):
    key_ref, value_ref = refs[-2:]
    rows_dev = key_ref.shape[1]
    for pair in range(SPREAD_PAIRS):
        head = 2 * (SPREAD_PAIRS * pl.program_id(0) + pair)
        at = lanes(pair)
        key_rows, value_rows, used = [], [], 0
        for level, blocks in levels:
            count = rows_dev >> (level + 1)
            total = sum(ref[:, at].astype(F32) for ref in refs[used : used + blocks])
            used += blocks
            key_rows.append(total[:count])
            value_rows.append(total[count:])
        both = jnp.concatenate(
            [jnp.concatenate(key_rows, axis=0), jnp.concatenate(value_rows, axis=0)], axis=1
        ).astype(BF16)
        spread = [
            jnp.dot(
                selection(offsets_ref, head + side, rows_dev, [level for level, _ in levels], True),
                both,
                preferred_element_type=F32,
            )
            for side in range(2)
        ]
        low, _ = lane_masks(rows_dev)
        for half, (base_ref, ref) in enumerate(((key_base_ref, key_ref), (value_base_ref, value_ref))):
            columns = slice(half * PAIR, (half + 1) * PAIR)
            ref[0, :, at] = (
                base_ref[0, :, at] + jnp.where(low, spread[0][:, columns], spread[1][:, columns])
            ).astype(ref.dtype)


def spread(offsets, base, levels, kind):
    key_base, value_base = base
    rows_dev, feature = key_base.shape[1:]
    width = SPREAD_PAIRS * PAIR
    blocks, specs = [], []
    for level, parts in levels:
        rows = 2 * (rows_dev >> (level + 1))
        for block, start in parts:
            blocks.append(block)
            specs.append(pl.BlockSpec((rows, width), functools.partial(lambda first, i: (first, i), start // rows)))
    out = pl.BlockSpec((1, rows_dev, width), lambda i: (0, 0, i))
    shape = jax.ShapeDtypeStruct((1, rows_dev, feature), kind)
    return pl.pallas_call(
        functools.partial(spread_kernel, [(level, len(parts)) for level, parts in levels]),
        grid=(feature // width,),
        in_specs=[
            pl.BlockSpec(memory_space=pltpu.SMEM),
            pl.BlockSpec((1, rows_dev, width), lambda i: (0, 0, i)),
            pl.BlockSpec((1, rows_dev, width), lambda i: (int(key_base is value_base), 0, i)),
        ]
        + specs,
        out_specs=[out, out],
        out_shape=[shape, shape],
        compiler_params=pltpu.CompilerParams(vmem_limit_bytes=VMEM_LIMIT),
        cost_estimate=pl.CostEstimate(flops=2 * CORE_RATE, bytes_accessed=4 * 10**6, transcendentals=0),
        name="spread_rows",
    )(offsets, key_base, value_base, *blocks)


def swap(block, bits):
    return lax.ppermute(block, "seq", [(i, i ^ bits) for i in range(lax.axis_size("seq"))])


def slide_swap(block, bits):
    return lax.ppermute(block, "dp", [(i, i ^ bits) for i in range(lax.axis_size("dp"))])


def after(block, others):
    tied = lax.optimization_barrier((block,) + tuple(others))
    return tied[0], list(tied[1:])


def plane_share(cotangent, attended):
    core = lax.axis_index("dp") % 2
    half = attended.shape[1] // 2

    def columns(which):
        block = lax.dynamic_slice_in_dim(attended, which * half, half, 1)
        return lax.dot_general(cotangent, block, (((0,), (0,)), ((), ())), preferred_element_type=F32)

    sent = slide_swap(columns(1 - core).astype(BF16), 1)
    total = (columns(core) + sent.astype(F32)).astype(BF16)
    planes = lax.axis_size("seq") // RUN
    groups = [[RUN * place + z for place in range(planes)] for z in range(RUN)]
    shares = lax.all_to_all(total, "seq", 0, 0, axis_index_groups=groups, tiled=True)
    return jnp.sum(shares.reshape(planes, -1, half).astype(F32), axis=0).astype(BF16), sent


def slides_total(share, norm_factor, others):
    mine = ((share.astype(F32) + slide_swap(share, 2).astype(F32)) * norm_factor).astype(BF16)
    mine, others = after(mine, others)
    other = slide_swap(mine, 1)
    half = mine.shape[1] // 2
    low = lax.axis_index("dp") % 2 == 0
    left, right = jnp.where(low, mine, other), jnp.where(low, other, mine)
    rows = [jnp.concatenate([left[:, at], right[:, at]], axis=1) for at in (slice(0, half), slice(half, None))]
    whole = jnp.concatenate(rows, axis=0)
    return whole, others


def shards(queries, keys, values, out_weight, out_cotangent, offsets):
    rows_dev, feature = queries.shape[1:]
    cotangent = out_cotangent[0]
    n3 = rows_dev // 4
    far, near, mid = pick(offsets, keys, values)
    fars = [far] + [swap(far, bits) for bits in (1, 2, 3)]
    cross = swap(jnp.concatenate(fars, axis=0), 4)
    near_pair, mid2, mid3 = swap(near, 1), swap(mid, 2), swap(mid, 3)
    grads = jnp.dot(cotangent, out_weight, preferred_element_type=F32).astype(BF16)
    gathered = [near_pair, mid2, mid3] + fars + [cross]
    own_parts = attend_own(GROUPS[0], queries, keys, values, near, mid, far)
    results = attend_both(GROUPS[0], queries, keys, values, grads, near, mid, gathered, own_parts)
    attended, query_grad, local, own1, own2, far_grad, back = results[:7]
    cross_back = swap(back, 4)
    back1, back2, back3 = [swap(block, bits) for bits, block in zip((1, 2, 3), results[7:])]
    mixed = lax.dot_general(
        attended, out_weight, (((1,), (1,)), ((), ())), preferred_element_type=F32
    ).astype(BF16)
    share, sent = plane_share(cotangent, attended)
    share, (mixed,) = after(share, [mixed])
    far_grad, (back1, back2) = after(far_grad, [back1, back2])
    far_grad = (far_grad.astype(F32) + cross_back.astype(F32)).astype(BF16)
    far_parts = [far_grad[bits * n3 : (bits + 1) * n3] for bits in range(4)]
    rows, half = share.shape[0] // RUN, share.shape[1]
    place = lax.axis_index("seq") % RUN
    packed = rows // 2
    share_parts = []
    for bits in range(4):
        part = lax.dynamic_slice_in_dim(share, (place ^ bits) * rows, rows, 0)
        share_parts.append(jnp.concatenate([part[:packed], part[packed:]], axis=1))
    total = share_parts[0].astype(F32)
    far_back = []
    for bits in (1, 2, 3):
        padded = jnp.pad(share_parts[bits], ((0, -packed % 8), (0, feature - 2 * half)))
        arrived = swap(jnp.concatenate([far_parts[bits], padded], axis=0), bits)
        far_back.append(arrived)
        total = total + arrived[n3 : n3 + packed, : 2 * half].astype(F32)
    tiles = lax.axis_size("dp") * lax.axis_size("seq") * rows_dev
    local = local.reshape(2, rows_dev, feature)
    base = spread(
        offsets,
        (local, local),
        ((0, ((own1, 0), (back1, 0))), (1, ((own2, 0), (back1, rows_dev), (back2, 0), (back3, 0)))),
        F32,
    )
    total, base = after(total.astype(BF16), base)
    key_grad, value_grad = spread(
        offsets, base, ((2, tuple((block, 0) for block in [far_grad] + far_back)),), BF16
    )
    weight_grad, (key_grad, value_grad) = slides_total(
        total, 1.0 / math.sqrt(tiles), [key_grad, value_grad]
    )
    return mixed[None], query_grad, key_grad, value_grad, weight_grad


def solution(mesh):
    split = P("dp", "seq", None)
    return jax.shard_map(
        shards,
        mesh=mesh,
        in_specs=(split, split, split, P(), split, P()),
        out_specs=(split, split, split, split, P("seq", None)),
        check_vma=False,
    )
```

```python
import functools
import math

import jax
import jax.numpy as jnp
from jax import lax
from jax.experimental import pallas as pl
from jax.experimental.pallas import tpu as pltpu
from jax.sharding import PartitionSpec as P

HEADS = 12
HEAD_DIM = 64
LEVELS = 3
PAIR = 2 * HEAD_DIM
VMEM_LIMIT = 60 * 1024 * 1024
LOG2E = 1.0 / math.log(2.0)
GROUPS = ((0, HEADS // 2),)
PICK_PAIRS = 3
SPREAD_PAIRS = 3
CORE_RATE = 10**9
RUN = 4
F32 = jnp.float32
BF16 = jnp.bfloat16


def lane_masks(row_count):
    lane = lax.broadcasted_iota(jnp.int32, (row_count, PAIR), 1)
    return lane < HEAD_DIM, lane >= HEAD_DIM


def selection(offsets_ref, head, rows_dev, levels, transposed):
    counts = [rows_dev >> (level + 1) for level in levels]
    shape = (rows_dev, sum(counts)) if transposed else (sum(counts), rows_dev)
    slot = lax.broadcasted_iota(jnp.int32, shape, 1 if transposed else 0)
    row = lax.broadcasted_iota(jnp.int32, shape, 0 if transposed else 1)
    target, start = None, 0
    for level, count in zip(levels, counts):
        found = (2 << level) * (slot - start) + offsets_ref[level, head]
        target = found if target is None else jnp.where(slot < start, target, found)
        start += count
    return (row == target).astype(F32).astype(BF16)


def lanes(pair):
    return slice(pair * PAIR, (pair + 1) * PAIR)


def pick_kernel(offsets_ref, key_ref, value_ref, far_ref, near_ref, mid_ref):
    rows_dev = key_ref.shape[1]
    n1, n2, n3 = rows_dev // 2, rows_dev // 4, rows_dev // 8
    for pair in range(PICK_PAIRS):
        head = 2 * (PICK_PAIRS * pl.program_id(0) + pair)
        at = lanes(pair)
        both = jnp.concatenate([key_ref[0, :, at], value_ref[0, :, at]], axis=1)
        rows = [
            jnp.dot(selection(offsets_ref, head + side, rows_dev, (0, 1, 2), False), both, preferred_element_type=F32)
            for side in range(2)
        ]
        low, _ = lane_masks(rows[0].shape[0])
        key_rows = jnp.where(low, rows[0][:, :PAIR], rows[1][:, :PAIR]).astype(BF16)
        value_rows = jnp.where(low, rows[0][:, PAIR:], rows[1][:, PAIR:]).astype(BF16)
        near_ref[:n1, at] = key_rows[:n1]
        near_ref[n1 : 2 * n1, at] = value_rows[:n1]
        near_ref[2 * n1 : 2 * n1 + n2, at] = key_rows[n1 : n1 + n2]
        near_ref[2 * n1 + n2 :, at] = value_rows[n1 : n1 + n2]
        mid_ref[:n2, at] = key_rows[n1 : n1 + n2]
        mid_ref[n2:, at] = value_rows[n1 : n1 + n2]
        far_ref[:n3, at] = key_rows[n1 + n2 :]
        far_ref[n3:, at] = value_rows[n1 + n2 :]


def pick(offsets, keys, values):
    rows_dev, feature = keys.shape[1:]
    width = PICK_PAIRS * PAIR
    whole = pl.BlockSpec((1, rows_dev, width), lambda i: (0, 0, i))
    rows = (rows_dev // 4, 3 * rows_dev // 2, rows_dev // 2)
    return pl.pallas_call(
        pick_kernel,
        grid=(feature // width,),
        in_specs=[pl.BlockSpec(memory_space=pltpu.SMEM), whole, whole],
        out_specs=[pl.BlockSpec((count, width), lambda i: (0, i)) for count in rows],
        out_shape=[jax.ShapeDtypeStruct((count, feature), BF16) for count in rows],
        compiler_params=pltpu.CompilerParams(vmem_limit_bytes=VMEM_LIMIT),
        cost_estimate=pl.CostEstimate(flops=2 * CORE_RATE, bytes_accessed=2 * 10**6, transcendentals=0),
        name="pick_rows",
    )(offsets, keys, values)


def sides(block):
    return [jnp.where(mask, block, jnp.zeros_like(block)) for mask in lane_masks(block.shape[0])]


def head_rows(side):
    return slice(side * HEAD_DIM, (side + 1) * HEAD_DIM)


NT = (((1,), (1,)), ((), ()))


def copy_rows(key_set, value_set, key_ref, value_ref, sources):
    at = 0
    if key_ref is not None:
        at = key_ref.shape[1]
        key_set[:at] = key_ref[0]
        value_set[:at] = value_ref[0]
    for ref, base, count in sources:
        key_set[at : at + count] = ref[base : base + count]
        value_set[at : at + count] = ref[base + count : base + 2 * count]
        at += count


def level_rows(rows_dev):
    return rows_dev // 2, rows_dev // 4, rows_dev // 8


def scaled_sides(query_ref):
    return sides((query_ref[0].astype(F32) * (1.0 / math.sqrt(HEAD_DIM))).astype(BF16))


def scores_of(keys, query_side):
    return lax.dot_general(keys, query_side, NT, preferred_element_type=F32)


def own_kernel(query_ref, key_ref, value_ref, near_ref, mid_ref, far_ref, raw_ref, stats_ref, part_ref, key_set, value_set):
    n1, n2, n3 = level_rows(query_ref.shape[1])
    copy_rows(key_set, value_set, key_ref, value_ref, [(near_ref, 0, n1), (mid_ref, 0, n2), (far_ref, 0, n3)])
    values_t = value_set[...].T
    rows_dev = query_ref.shape[1]
    for side, query_side in enumerate(scaled_sides(query_ref)):
        scores = scores_of(key_set[...], query_side)
        row_max = jnp.max(scores, axis=0, keepdims=True)
        weights = jnp.exp2(scores * LOG2E - row_max * LOG2E)
        raw = weights.astype(BF16)
        raw_ref[0, :, side * rows_dev : (side + 1) * rows_dev] = raw
        total = jnp.sum(weights, axis=0, keepdims=True)
        for place, row in enumerate((row_max, total)):
            first = 16 * side + 8 * place
            stats_ref[0, first : first + 8] = jnp.broadcast_to(row, (8, rows_dev))
        part_ref[0, head_rows(side)] = jnp.dot(values_t[head_rows(side)], raw, preferred_element_type=F32)


def both_kernel(query_ref, key_ref, value_ref, near_ref, *refs):
    (near_pair_ref, mid2_ref, mid3_ref, far0_ref, far1_ref, far2_ref, far3_ref, cross_ref,
     grad_ref, mid_ref, own_raw_ref, stats_ref, part_ref) = refs[:13]
    attended_ref, query_grad_ref = refs[13:15]
    local_ref, own1_ref, own2_ref, far_ref, back_ref, send1_ref, send2_ref, send3_ref = refs[15:-2]
    key_set, value_set = refs[-2:]
    rows_dev = query_ref.shape[1]
    n1, n2, n3 = level_rows(rows_dev)
    own = rows_dev + n1 + n2 + n3
    copy_rows(
        key_set, value_set, key_ref, value_ref,
        [(near_ref, 0, n1), (mid_ref, 0, n2), (far0_ref, 0, n3)]
        + [(near_pair_ref, 0, n1), (near_pair_ref, 2 * n1, n2), (mid2_ref, 0, n2), (mid3_ref, 0, n2)]
        + [(ref, 0, n3) for ref in (far1_ref, far2_ref, far3_ref)]
        + [(cross_ref, 2 * n3 * idx, n3) for idx in range(4)],
    )
    query_sides = scaled_sides(query_ref)
    scores = [scores_of(key_set[own:], side) for side in query_sides]
    far_values_t = value_set[own:].T
    raw, scales, attended_t = [], [], []
    for side in range(2):
        own_max, own_sum = (stats_ref[0, first : first + 1] for first in (16 * side, 16 * side + 8))
        row_max = jnp.maximum(own_max, jnp.max(scores[side], axis=0, keepdims=True))
        weights = jnp.exp2(scores[side] * LOG2E - row_max * LOG2E)
        own_factor = jnp.exp2((own_max - row_max) * LOG2E)
        inverse = 1.0 / (own_sum * own_factor + jnp.sum(weights, axis=0, keepdims=True))
        raw.append(weights.astype(BF16))
        scales.append((inverse * own_factor, inverse))
        rows = head_rows(side)
        product = jnp.dot(far_values_t[rows], raw[side], preferred_element_type=F32)
        attended_t.append(((part_ref[0, rows] * own_factor + product) * inverse).astype(BF16))
    attended_ref[...] = jnp.concatenate(attended_t, axis=0).T

    grad_t = grad_ref[...].T.astype(F32)
    own_raw = own_raw_ref[0]
    raws = [(own_raw[:, side * rows_dev : (side + 1) * rows_dev], raw[side]) for side in range(2)]
    score_grads = [[], []]
    value_sums = []
    for part, values in enumerate((value_set[:own], value_set[own:])):
        normed = [(grad_t[head_rows(side)] * scales[side][part]).astype(BF16) for side in range(2)]
        grad_sides = sides(jnp.concatenate(normed, axis=0).T)
        for side in range(2):
            prob_grad = scores_of(values, grad_sides[side])
            delta = jnp.sum(normed[side].astype(F32) * attended_t[side].astype(F32), axis=0, keepdims=True)
            score_grads[side].append((raws[side][part].astype(F32) * (prob_grad - delta)).astype(BF16))
        pair = own_raw if part == 0 else jnp.concatenate(raw, axis=1)
        value_sums.append(jnp.dot(pair, jnp.concatenate(grad_sides, axis=0), preferred_element_type=F32))
    value_sum = jnp.concatenate(value_sums, axis=0)
    score_grads = [jnp.concatenate(parts, axis=0) for parts in score_grads]
    keys_t = key_set[...].T
    query_t = jnp.concatenate(
        [jnp.dot(keys_t[head_rows(side)], score_grads[side], preferred_element_type=F32) for side in range(2)],
        axis=0,
    )
    query_grad_ref[0] = (query_t * (1.0 / math.sqrt(HEAD_DIM))).astype(BF16).T
    key_sum = jnp.dot(
        jnp.concatenate(score_grads, axis=1), jnp.concatenate(query_sides, axis=0), preferred_element_type=F32
    )
    targets = [(local_ref, 0, rows_dev), (own1_ref, 0, n1), (own2_ref, 0, n2), (far_ref, 0, n3)]
    targets += [(send1_ref, 0, n1), (send1_ref, 2 * n1, n2), (send2_ref, 0, n2), (send3_ref, 0, n2)]
    targets += [(far_ref, 2 * n3 * idx, n3) for idx in range(1, 4)]
    targets += [(back_ref, 2 * n3 * idx, n3) for idx in range(4)]
    at = 0
    for ref, base, count in targets:
        ref[base : base + count] = key_sum[at : at + count].astype(ref.dtype)
        ref[base + count : base + 2 * count] = value_sum[at : at + count].astype(ref.dtype)
        at += count


class Layout:
    def __init__(self, group, rows_dev, feature):
        self.first, self.count = group
        self.rows_dev, self.feature, self.width = rows_dev, feature, group[1] * PAIR
        self.set_rows = 4 * rows_dev
        self.given = pl.BlockSpec((1, rows_dev, PAIR), lambda i: (0, 0, group[0] + i))
        self.sets = [pltpu.VMEM((self.set_rows, PAIR), BF16)] * 2

    def whole(self, rows):
        return pl.BlockSpec((rows, PAIR), lambda i: (0, self.first + i))

    def part(self, rows):
        return pl.BlockSpec((rows, PAIR), lambda i: (0, i))

    def stacked(self, block):
        return pl.BlockSpec((1,) + block.shape[1:], lambda i: (i, 0, 0))

    def of(self, block):
        return self.part(block.shape[0]) if block.shape[1] == self.width else self.whole(block.shape[0])

    def gradient_outs(self):
        rows, shape = self.rows_dev, jax.ShapeDtypeStruct
        wide = [(2 * rows, F32), (rows, F32), (rows // 2, F32), (rows, BF16)]
        narrow = [rows, 3 * rows // 2, rows // 2, rows // 2]
        specs = [self.given] + [self.whole(count) for count, _ in wide] + [self.part(count) for count in narrow]
        shapes = [shape((1, rows, self.feature), BF16)]
        shapes += [shape((count, self.feature), kind) for count, kind in wide]
        shapes += [shape((count, self.width), BF16) for count in narrow]
        return specs, shapes

    def call(self, kernel, name, operands, in_specs, out_specs, out_shapes, scratch, micros, before=()):
        return pl.pallas_call(
            kernel,
            grid=(self.count,),
            in_specs=list(in_specs) + [pl.BlockSpec(memory_space=pl.ANY)] * len(before),
            out_specs=out_specs,
            out_shape=out_shapes,
            input_output_aliases={len(operands) + idx: idx for idx in range(len(before))},
            scratch_shapes=scratch,
            compiler_params=pltpu.CompilerParams(vmem_limit_bytes=VMEM_LIMIT),
            cost_estimate=pl.CostEstimate(
                flops=int(micros * self.count * CORE_RATE), bytes_accessed=10**6, transcendentals=0
            ),
            name=name,
        )(*operands, *before)


def attend_own(group, queries, keys, values, near, mid, far):
    rows_dev, feature = queries.shape[1:]
    lay = Layout(group, rows_dev, feature)
    own = rows_dev + sum(level_rows(rows_dev))
    shape = jax.ShapeDtypeStruct
    shapes = [
        shape((lay.count, own, 2 * rows_dev), BF16),
        shape((lay.count, 32, rows_dev), F32),
        shape((lay.count, PAIR, rows_dev), F32),
    ]
    operands = (queries, keys, values, near, mid, far)
    return lay.call(
        own_kernel, "attend_own", operands, [lay.given] * 3 + [lay.of(block) for block in operands[3:]],
        [lay.stacked(out) for out in shapes], shapes, [pltpu.VMEM((own, PAIR), BF16)] * 2, 0.1,
    )


def attend_both(group, queries, keys, values, grads, near, mid, gathered, own_parts):
    rows_dev, feature = queries.shape[1:]
    lay = Layout(group, rows_dev, feature)
    specs, shapes = lay.gradient_outs()
    operands = (queries, keys, values, near) + tuple(gathered) + (grads, mid) + tuple(own_parts)
    return lay.call(
        both_kernel, "attend_both", operands,
        [lay.given] * 3 + [lay.of(block) for block in operands[3:-3]] + [lay.stacked(block) for block in own_parts],
        [lay.whole(rows_dev)] + specs, [jax.ShapeDtypeStruct((rows_dev, feature), BF16)] + shapes,
        lay.sets, 2.6,
    )


def spread_kernel(levels, offsets_ref, key_base_ref, value_base_ref, *refs):
    key_ref, value_ref = refs[-2:]
    rows_dev = key_ref.shape[1]
    for pair in range(SPREAD_PAIRS):
        head = 2 * (SPREAD_PAIRS * pl.program_id(0) + pair)
        at = lanes(pair)
        key_rows, value_rows, used = [], [], 0
        for level, blocks in levels:
            count = rows_dev >> (level + 1)
            total = sum(ref[:, at].astype(F32) for ref in refs[used : used + blocks])
            used += blocks
            key_rows.append(total[:count])
            value_rows.append(total[count:])
        both = jnp.concatenate(
            [jnp.concatenate(key_rows, axis=0), jnp.concatenate(value_rows, axis=0)], axis=1
        ).astype(BF16)
        spread = [
            jnp.dot(
                selection(offsets_ref, head + side, rows_dev, [level for level, _ in levels], True),
                both,
                preferred_element_type=F32,
            )
            for side in range(2)
        ]
        low, _ = lane_masks(rows_dev)
        for half, (base_ref, ref) in enumerate(((key_base_ref, key_ref), (value_base_ref, value_ref))):
            columns = slice(half * PAIR, (half + 1) * PAIR)
            ref[0, :, at] = (
                base_ref[0, :, at] + jnp.where(low, spread[0][:, columns], spread[1][:, columns])
            ).astype(ref.dtype)


def spread(offsets, base, levels, kind):
    key_base, value_base = base
    rows_dev, feature = key_base.shape[1:]
    width = SPREAD_PAIRS * PAIR
    blocks, specs = [], []
    for level, parts in levels:
        rows = 2 * (rows_dev >> (level + 1))
        for block, start in parts:
            blocks.append(block)
            specs.append(pl.BlockSpec((rows, width), functools.partial(lambda first, i: (first, i), start // rows)))
    out = pl.BlockSpec((1, rows_dev, width), lambda i: (0, 0, i))
    shape = jax.ShapeDtypeStruct((1, rows_dev, feature), kind)
    return pl.pallas_call(
        functools.partial(spread_kernel, [(level, len(parts)) for level, parts in levels]),
        grid=(feature // width,),
        in_specs=[
            pl.BlockSpec(memory_space=pltpu.SMEM),
            pl.BlockSpec((1, rows_dev, width), lambda i: (0, 0, i)),
            pl.BlockSpec((1, rows_dev, width), lambda i: (int(key_base is value_base), 0, i)),
        ]
        + specs,
        out_specs=[out, out],
        out_shape=[shape, shape],
        compiler_params=pltpu.CompilerParams(vmem_limit_bytes=VMEM_LIMIT),
        cost_estimate=pl.CostEstimate(flops=2 * CORE_RATE, bytes_accessed=4 * 10**6, transcendentals=0),
        name="spread_rows",
    )(offsets, key_base, value_base, *blocks)


def swap(block, bits):
    return lax.ppermute(block, "seq", [(i, i ^ bits) for i in range(lax.axis_size("seq"))])


def slide_swap(block, bits):
    return lax.ppermute(block, "dp", [(i, i ^ bits) for i in range(lax.axis_size("dp"))])


def after(block, others):
    tied = lax.optimization_barrier((block,) + tuple(others))
    return tied[0], list(tied[1:])


def plane_share(cotangent, attended):
    core = lax.axis_index("dp") % 2
    half = attended.shape[1] // 2

    def columns(which):
        block = lax.dynamic_slice_in_dim(attended, which * half, half, 1)
        return lax.dot_general(cotangent, block, (((0,), (0,)), ((), ())), preferred_element_type=F32)

    sent = slide_swap(columns(1 - core).astype(BF16), 1)
    total = (columns(core) + sent.astype(F32)).astype(BF16)
    planes = lax.axis_size("seq") // RUN
    groups = [[RUN * place + z for place in range(planes)] for z in range(RUN)]
    shares = lax.all_to_all(total, "seq", 0, 0, axis_index_groups=groups, tiled=True)
    return jnp.sum(shares.reshape(planes, -1, half).astype(F32), axis=0).astype(BF16), sent


def slides_total(share, norm_factor, others):
    mine = ((share.astype(F32) + slide_swap(share, 2).astype(F32)) * norm_factor).astype(BF16)
    mine, others = after(mine, others)
    other = slide_swap(mine, 1)
    half = mine.shape[1] // 2
    low = lax.axis_index("dp") % 2 == 0
    left, right = jnp.where(low, mine, other), jnp.where(low, other, mine)
    rows = [jnp.concatenate([left[:, at], right[:, at]], axis=1) for at in (slice(0, half), slice(half, None))]
    whole = jnp.concatenate(rows, axis=0)
    return whole, others


def shards(queries, keys, values, out_weight, out_cotangent, offsets):
    rows_dev, feature = queries.shape[1:]
    cotangent = out_cotangent[0]
    n3 = rows_dev // 4
    far, near, mid = pick(offsets, keys, values)
    fars = [far] + [swap(far, bits) for bits in (1, 2, 3)]
    cross = swap(jnp.concatenate(fars, axis=0), 4)
    near_pair, mid2, mid3 = swap(near, 1), swap(mid, 2), swap(mid, 3)
    late_cotangent, (mid2,) = after(cotangent, [mid2])
    grads = jnp.dot(late_cotangent, out_weight, preferred_element_type=F32).astype(BF16)
    gathered = [near_pair, mid2, mid3] + fars + [cross]
    own_parts = attend_own(GROUPS[0], queries, keys, values, near, mid, far)
    results = attend_both(GROUPS[0], queries, keys, values, grads, near, mid, gathered, own_parts)
    attended, query_grad, local, own1, own2, far_grad, back = results[:7]
    cross_back = swap(back, 4)
    back1, back2, back3 = [swap(block, bits) for bits, block in zip((1, 2, 3), results[7:])]
    mixed = lax.dot_general(
        attended, out_weight, (((1,), (1,)), ((), ())), preferred_element_type=F32
    ).astype(BF16)
    share, sent = plane_share(cotangent, attended)
    share, (mixed,) = after(share, [mixed])
    far_grad, (back1, back2) = after(far_grad, [back1, back2])
    far_grad = (far_grad.astype(F32) + cross_back.astype(F32)).astype(BF16)
    far_parts = [far_grad[bits * n3 : (bits + 1) * n3] for bits in range(4)]
    rows, half = share.shape[0] // RUN, share.shape[1]
    place = lax.axis_index("seq") % RUN
    packed = rows // 2
    share_parts = []
    for bits in range(4):
        part = lax.dynamic_slice_in_dim(share, (place ^ bits) * rows, rows, 0)
        share_parts.append(jnp.concatenate([part[:packed], part[packed:]], axis=1))
    total = share_parts[0].astype(F32)
    far_back = []
    for bits in (1, 2, 3):
        padded = jnp.pad(share_parts[bits], ((0, -packed % 8), (0, feature - 2 * half)))
        arrived = swap(jnp.concatenate([far_parts[bits], padded], axis=0), bits)
        far_back.append(arrived)
        total = total + arrived[n3 : n3 + packed, : 2 * half].astype(F32)
    tiles = lax.axis_size("dp") * lax.axis_size("seq") * rows_dev
    local = local.reshape(2, rows_dev, feature)
    base = spread(
        offsets,
        (local, local),
        ((0, ((own1, 0), (back1, 0))), (1, ((own2, 0), (back1, rows_dev), (back2, 0), (back3, 0)))),
        F32,
    )
    total, base = after(total.astype(BF16), base)
    key_grad, value_grad = spread(
        offsets, base, ((2, tuple((block, 0) for block in [far_grad] + far_back)),), BF16
    )
    weight_grad, (key_grad, value_grad) = slides_total(
        total, 1.0 / math.sqrt(tiles), [key_grad, value_grad]
    )
    return mixed[None], query_grad, key_grad, value_grad, weight_grad


def solution(mesh):
    split = P("dp", "seq", None)
    return jax.shard_map(
        shards,
        mesh=mesh,
        in_specs=(split, split, split, P(), split, P()),
        out_specs=(split, split, split, split, P("seq", None)),
        check_vma=False,
    )
```

```python
import functools
import math

import jax
import jax.numpy as jnp
from jax import lax
from jax.experimental import pallas as pl
from jax.experimental.layout import Layout as Order, with_layout_constraint
from jax.experimental.pallas import tpu as pltpu
from jax.sharding import PartitionSpec as P

HEADS = 12
HEAD_DIM = 64
LEVELS = 3
PAIR = 2 * HEAD_DIM
VMEM_LIMIT = 60 * 1024 * 1024
LOG2E = 1.0 / math.log(2.0)
GROUPS = ((0, HEADS // 2),)
PICK_PAIRS = 3
SPREAD_PAIRS = 3
CORE_RATE = 10**9
RUN = 4
F32 = jnp.float32
BF16 = jnp.bfloat16


def lane_masks(row_count):
    lane = lax.broadcasted_iota(jnp.int32, (row_count, PAIR), 1)
    return lane < HEAD_DIM, lane >= HEAD_DIM


def selection(offsets_ref, head, rows_dev, levels, transposed):
    counts = [rows_dev >> (level + 1) for level in levels]
    shape = (rows_dev, sum(counts)) if transposed else (sum(counts), rows_dev)
    slot = lax.broadcasted_iota(jnp.int32, shape, 1 if transposed else 0)
    row = lax.broadcasted_iota(jnp.int32, shape, 0 if transposed else 1)
    target, start = None, 0
    for level, count in zip(levels, counts):
        found = (2 << level) * (slot - start) + offsets_ref[level, head]
        target = found if target is None else jnp.where(slot < start, target, found)
        start += count
    return (row == target).astype(F32).astype(BF16)


def lanes(pair):
    return slice(pair * PAIR, (pair + 1) * PAIR)


def pick_kernel(offsets_ref, key_ref, value_ref, far_ref, near_ref, mid_ref):
    rows_dev = key_ref.shape[1]
    n1, n2, n3 = rows_dev // 2, rows_dev // 4, rows_dev // 8
    for pair in range(PICK_PAIRS):
        head = 2 * (PICK_PAIRS * pl.program_id(0) + pair)
        at = lanes(pair)
        both = jnp.concatenate([key_ref[0, :, at], value_ref[0, :, at]], axis=1)
        rows = [
            jnp.dot(selection(offsets_ref, head + side, rows_dev, (0, 1, 2), False), both, preferred_element_type=F32)
            for side in range(2)
        ]
        low, _ = lane_masks(rows[0].shape[0])
        key_rows = jnp.where(low, rows[0][:, :PAIR], rows[1][:, :PAIR]).astype(BF16)
        value_rows = jnp.where(low, rows[0][:, PAIR:], rows[1][:, PAIR:]).astype(BF16)
        near_ref[:n1, at] = key_rows[:n1]
        near_ref[n1 : 2 * n1, at] = value_rows[:n1]
        near_ref[2 * n1 : 2 * n1 + n2, at] = key_rows[n1 : n1 + n2]
        near_ref[2 * n1 + n2 :, at] = value_rows[n1 : n1 + n2]
        mid_ref[:n2, at] = key_rows[n1 : n1 + n2]
        mid_ref[n2:, at] = value_rows[n1 : n1 + n2]
        far_ref[:n3, at] = key_rows[n1 + n2 :]
        far_ref[n3:, at] = value_rows[n1 + n2 :]


def pick(offsets, keys, values):
    rows_dev, feature = keys.shape[1:]
    width = PICK_PAIRS * PAIR
    whole = pl.BlockSpec((1, rows_dev, width), lambda i: (0, 0, i))
    rows = (rows_dev // 4, 3 * rows_dev // 2, rows_dev // 2)
    return pl.pallas_call(
        pick_kernel,
        grid=(feature // width,),
        in_specs=[pl.BlockSpec(memory_space=pltpu.SMEM), whole, whole],
        out_specs=[pl.BlockSpec((count, width), lambda i: (0, i)) for count in rows],
        out_shape=[jax.ShapeDtypeStruct((count, feature), BF16) for count in rows],
        compiler_params=pltpu.CompilerParams(vmem_limit_bytes=VMEM_LIMIT),
        cost_estimate=pl.CostEstimate(flops=2 * CORE_RATE, bytes_accessed=2 * 10**6, transcendentals=0),
        name="pick_rows",
    )(offsets, keys, values)


def sides(block):
    return [jnp.where(mask, block, jnp.zeros_like(block)) for mask in lane_masks(block.shape[0])]


def head_rows(side):
    return slice(side * HEAD_DIM, (side + 1) * HEAD_DIM)


NT = (((1,), (1,)), ((), ()))


def copy_rows(key_set, value_set, key_ref, value_ref, sources):
    at = 0
    if key_ref is not None:
        at = key_ref.shape[1]
        key_set[:at] = key_ref[0]
        value_set[:at] = value_ref[0]
    for ref, base, count in sources:
        key_set[at : at + count] = ref[base : base + count]
        value_set[at : at + count] = ref[base + count : base + 2 * count]
        at += count


def level_rows(rows_dev):
    return rows_dev // 2, rows_dev // 4, rows_dev // 8


def scaled_sides(query_ref):
    return sides((query_ref[0].astype(F32) * (1.0 / math.sqrt(HEAD_DIM))).astype(BF16))


def scores_of(keys, query_side):
    return lax.dot_general(keys, query_side, NT, preferred_element_type=F32)


def own_kernel(query_ref, key_ref, value_ref, near_ref, mid_ref, far_ref, raw_ref, stats_ref, part_ref, key_set, value_set):
    n1, n2, n3 = level_rows(query_ref.shape[1])
    copy_rows(key_set, value_set, key_ref, value_ref, [(near_ref, 0, n1), (mid_ref, 0, n2), (far_ref, 0, n3)])
    values_t = value_set[...].T
    rows_dev = query_ref.shape[1]
    for side, query_side in enumerate(scaled_sides(query_ref)):
        scores = scores_of(key_set[...], query_side)
        row_max = jnp.max(scores, axis=0, keepdims=True)
        weights = jnp.exp2(scores * LOG2E - row_max * LOG2E)
        raw = weights.astype(BF16)
        raw_ref[0, :, side * rows_dev : (side + 1) * rows_dev] = raw
        total = jnp.sum(weights, axis=0, keepdims=True)
        for place, row in enumerate((row_max, total)):
            first = 16 * side + 8 * place
            stats_ref[0, first : first + 8] = jnp.broadcast_to(row, (8, rows_dev))
        part_ref[0, head_rows(side)] = jnp.dot(values_t[head_rows(side)], raw, preferred_element_type=F32)


def both_kernel(query_ref, key_ref, value_ref, near_ref, *refs):
    (near_pair_ref, mid2_ref, mid3_ref, far0_ref, far1_ref, far2_ref, far3_ref, cross_ref,
     grad_ref, mid_ref, own_raw_ref, stats_ref, part_ref) = refs[:13]
    attended_ref, query_grad_ref = refs[13:15]
    local_ref, own1_ref, own2_ref, far_ref, back_ref, send1_ref, send2_ref, send3_ref = refs[15:-2]
    key_set, value_set = refs[-2:]
    rows_dev = query_ref.shape[1]
    n1, n2, n3 = level_rows(rows_dev)
    own = rows_dev + n1 + n2 + n3
    copy_rows(
        key_set, value_set, key_ref, value_ref,
        [(near_ref, 0, n1), (mid_ref, 0, n2), (far0_ref, 0, n3)]
        + [(near_pair_ref, 0, n1), (near_pair_ref, 2 * n1, n2), (mid2_ref, 0, n2), (mid3_ref, 0, n2)]
        + [(ref, 0, n3) for ref in (far1_ref, far2_ref, far3_ref)]
        + [(cross_ref, 2 * n3 * idx, n3) for idx in range(4)],
    )
    query_sides = scaled_sides(query_ref)
    scores = [scores_of(key_set[own:], side) for side in query_sides]
    far_values_t = value_set[own:].T
    raw, scales, attended_t = [], [], []
    for side in range(2):
        own_max, own_sum = (stats_ref[0, first : first + 1] for first in (16 * side, 16 * side + 8))
        row_max = jnp.maximum(own_max, jnp.max(scores[side], axis=0, keepdims=True))
        weights = jnp.exp2(scores[side] * LOG2E - row_max * LOG2E)
        own_factor = jnp.exp2((own_max - row_max) * LOG2E)
        inverse = 1.0 / (own_sum * own_factor + jnp.sum(weights, axis=0, keepdims=True))
        raw.append(weights.astype(BF16))
        scales.append((inverse * own_factor, inverse))
        rows = head_rows(side)
        product = jnp.dot(far_values_t[rows], raw[side], preferred_element_type=F32)
        attended_t.append(((part_ref[0, rows] * own_factor + product) * inverse).astype(BF16))
    attended_ref[...] = jnp.concatenate(attended_t, axis=0).T

    grad_t = grad_ref[...].T.astype(F32)
    own_raw = own_raw_ref[0]
    raws = [(own_raw[:, side * rows_dev : (side + 1) * rows_dev], raw[side]) for side in range(2)]
    score_grads = [[], []]
    value_sums = []
    for part, values in enumerate((value_set[:own], value_set[own:])):
        normed = [(grad_t[head_rows(side)] * scales[side][part]).astype(BF16) for side in range(2)]
        grad_sides = sides(jnp.concatenate(normed, axis=0).T)
        for side in range(2):
            prob_grad = scores_of(values, grad_sides[side])
            delta = jnp.sum(normed[side].astype(F32) * attended_t[side].astype(F32), axis=0, keepdims=True)
            score_grads[side].append((raws[side][part].astype(F32) * (prob_grad - delta)).astype(BF16))
        pair = own_raw if part == 0 else jnp.concatenate(raw, axis=1)
        value_sums.append(jnp.dot(pair, jnp.concatenate(grad_sides, axis=0), preferred_element_type=F32))
    value_sum = jnp.concatenate(value_sums, axis=0)
    score_grads = [jnp.concatenate(parts, axis=0) for parts in score_grads]
    keys_t = key_set[...].T
    query_t = jnp.concatenate(
        [jnp.dot(keys_t[head_rows(side)], score_grads[side], preferred_element_type=F32) for side in range(2)],
        axis=0,
    )
    query_grad_ref[0] = (query_t * (1.0 / math.sqrt(HEAD_DIM))).astype(BF16).T
    key_sum = jnp.dot(
        jnp.concatenate(score_grads, axis=1), jnp.concatenate(query_sides, axis=0), preferred_element_type=F32
    )
    targets = [(local_ref, 0, rows_dev), (own1_ref, 0, n1), (own2_ref, 0, n2), (far_ref, 0, n3)]
    targets += [(send1_ref, 0, n1), (send1_ref, 2 * n1, n2), (send2_ref, 0, n2), (send3_ref, 0, n2)]
    targets += [(far_ref, 2 * n3 * idx, n3) for idx in range(1, 4)]
    targets += [(back_ref, 2 * n3 * idx, n3) for idx in range(4)]
    at = 0
    for ref, base, count in targets:
        ref[base : base + count] = key_sum[at : at + count].astype(ref.dtype)
        ref[base + count : base + 2 * count] = value_sum[at : at + count].astype(ref.dtype)
        at += count


class Layout:
    def __init__(self, group, rows_dev, feature):
        self.first, self.count = group
        self.rows_dev, self.feature, self.width = rows_dev, feature, group[1] * PAIR
        self.set_rows = 4 * rows_dev
        self.given = pl.BlockSpec((1, rows_dev, PAIR), lambda i: (0, 0, group[0] + i))
        self.sets = [pltpu.VMEM((self.set_rows, PAIR), BF16)] * 2

    def whole(self, rows):
        return pl.BlockSpec((rows, PAIR), lambda i: (0, self.first + i))

    def part(self, rows):
        return pl.BlockSpec((rows, PAIR), lambda i: (0, i))

    def stacked(self, block):
        return pl.BlockSpec((1,) + block.shape[1:], lambda i: (i, 0, 0))

    def of(self, block):
        return self.part(block.shape[0]) if block.shape[1] == self.width else self.whole(block.shape[0])

    def gradient_outs(self):
        rows, shape = self.rows_dev, jax.ShapeDtypeStruct
        wide = [(2 * rows, F32), (rows, F32), (rows // 2, F32), (rows, BF16)]
        narrow = [rows, 3 * rows // 2, rows // 2, rows // 2]
        specs = [self.given] + [self.whole(count) for count, _ in wide] + [self.part(count) for count in narrow]
        shapes = [shape((1, rows, self.feature), BF16)]
        shapes += [shape((count, self.feature), kind) for count, kind in wide]
        shapes += [shape((count, self.width), BF16) for count in narrow]
        return specs, shapes

    def call(self, kernel, name, operands, in_specs, out_specs, out_shapes, scratch, micros, before=()):
        return pl.pallas_call(
            kernel,
            grid=(self.count,),
            in_specs=list(in_specs) + [pl.BlockSpec(memory_space=pl.ANY)] * len(before),
            out_specs=out_specs,
            out_shape=out_shapes,
            input_output_aliases={len(operands) + idx: idx for idx in range(len(before))},
            scratch_shapes=scratch,
            compiler_params=pltpu.CompilerParams(vmem_limit_bytes=VMEM_LIMIT),
            cost_estimate=pl.CostEstimate(
                flops=int(micros * self.count * CORE_RATE), bytes_accessed=10**6, transcendentals=0
            ),
            name=name,
        )(*operands, *before)


def attend_own(group, queries, keys, values, near, mid, far):
    rows_dev, feature = queries.shape[1:]
    lay = Layout(group, rows_dev, feature)
    own = rows_dev + sum(level_rows(rows_dev))
    shape = jax.ShapeDtypeStruct
    shapes = [
        shape((lay.count, own, 2 * rows_dev), BF16),
        shape((lay.count, 32, rows_dev), F32),
        shape((lay.count, PAIR, rows_dev), F32),
    ]
    operands = (queries, keys, values, near, mid, far)
    return lay.call(
        own_kernel, "attend_own", operands, [lay.given] * 3 + [lay.of(block) for block in operands[3:]],
        [lay.stacked(out) for out in shapes], shapes, [pltpu.VMEM((own, PAIR), BF16)] * 2, 0.1,
    )


def attend_both(group, queries, keys, values, grads, near, mid, gathered, own_parts):
    rows_dev, feature = queries.shape[1:]
    lay = Layout(group, rows_dev, feature)
    specs, shapes = lay.gradient_outs()
    operands = (queries, keys, values, near) + tuple(gathered) + (grads, mid) + tuple(own_parts)
    return lay.call(
        both_kernel, "attend_both", operands,
        [lay.given] * 3 + [lay.of(block) for block in operands[3:-3]] + [lay.stacked(block) for block in own_parts],
        [lay.whole(rows_dev)] + specs, [jax.ShapeDtypeStruct((rows_dev, feature), BF16)] + shapes,
        lay.sets, 2.6,
    )


def spread_kernel(levels, offsets_ref, key_base_ref, value_base_ref, *refs):
    key_ref, value_ref = refs[-2:]
    rows_dev = key_ref.shape[1]
    for pair in range(SPREAD_PAIRS):
        head = 2 * (SPREAD_PAIRS * pl.program_id(0) + pair)
        at = lanes(pair)
        key_rows, value_rows, used = [], [], 0
        for level, blocks in levels:
            count = rows_dev >> (level + 1)
            total = sum(ref[:, at].astype(F32) for ref in refs[used : used + blocks])
            used += blocks
            key_rows.append(total[:count])
            value_rows.append(total[count:])
        both = jnp.concatenate(
            [jnp.concatenate(key_rows, axis=0), jnp.concatenate(value_rows, axis=0)], axis=1
        ).astype(BF16)
        spread = [
            jnp.dot(
                selection(offsets_ref, head + side, rows_dev, [level for level, _ in levels], True),
                both,
                preferred_element_type=F32,
            )
            for side in range(2)
        ]
        low, _ = lane_masks(rows_dev)
        for half, (base_ref, ref) in enumerate(((key_base_ref, key_ref), (value_base_ref, value_ref))):
            columns = slice(half * PAIR, (half + 1) * PAIR)
            ref[0, :, at] = (
                base_ref[0, :, at] + jnp.where(low, spread[0][:, columns], spread[1][:, columns])
            ).astype(ref.dtype)


def spread(offsets, base, levels, kind):
    key_base, value_base = base
    rows_dev, feature = key_base.shape[1:]
    width = SPREAD_PAIRS * PAIR
    blocks, specs = [], []
    for level, parts in levels:
        rows = 2 * (rows_dev >> (level + 1))
        for block, start in parts:
            blocks.append(block)
            specs.append(pl.BlockSpec((rows, width), functools.partial(lambda first, i: (first, i), start // rows)))
    out = pl.BlockSpec((1, rows_dev, width), lambda i: (0, 0, i))
    shape = jax.ShapeDtypeStruct((1, rows_dev, feature), kind)
    return pl.pallas_call(
        functools.partial(spread_kernel, [(level, len(parts)) for level, parts in levels]),
        grid=(feature // width,),
        in_specs=[
            pl.BlockSpec(memory_space=pltpu.SMEM),
            pl.BlockSpec((1, rows_dev, width), lambda i: (0, 0, i)),
            pl.BlockSpec((1, rows_dev, width), lambda i: (int(key_base is value_base), 0, i)),
        ]
        + specs,
        out_specs=[out, out],
        out_shape=[shape, shape],
        compiler_params=pltpu.CompilerParams(vmem_limit_bytes=VMEM_LIMIT),
        cost_estimate=pl.CostEstimate(flops=2 * CORE_RATE, bytes_accessed=4 * 10**6, transcendentals=0),
        name="spread_rows",
    )(offsets, key_base, value_base, *blocks)


def swap(block, bits):
    return lax.ppermute(block, "seq", [(i, i ^ bits) for i in range(lax.axis_size("seq"))])


def slide_swap(block, bits):
    return lax.ppermute(block, "dp", [(i, i ^ bits) for i in range(lax.axis_size("dp"))])


def after(block, others):
    tied = lax.optimization_barrier((block,) + tuple(others))
    return tied[0], list(tied[1:])


def plane_share(cotangent, attended):
    core = lax.axis_index("dp") % 2
    half = attended.shape[1] // 2

    def columns(which):
        block = lax.dynamic_slice_in_dim(attended, which * half, half, 1)
        result = lax.dot_general(cotangent, block, (((0,), (0,)), ((), ())), preferred_element_type=F32)
        return with_layout_constraint(result, Order(major_to_minor=(0, 1)))

    sent = slide_swap(columns(1 - core).astype(BF16), 1)
    total = (columns(core) + sent.astype(F32)).astype(BF16)
    planes = lax.axis_size("seq") // RUN
    groups = [[RUN * place + z for place in range(planes)] for z in range(RUN)]
    shares = lax.all_to_all(total, "seq", 0, 0, axis_index_groups=groups, tiled=True)
    return jnp.sum(shares.reshape(planes, -1, half).astype(F32), axis=0).astype(BF16), sent


def slides_total(share, norm_factor, others):
    mine = ((share.astype(F32) + slide_swap(share, 2).astype(F32)) * norm_factor).astype(BF16)
    mine, others = after(mine, others)
    other = slide_swap(mine, 1)
    half = mine.shape[1] // 2
    low = lax.axis_index("dp") % 2 == 0
    left, right = jnp.where(low, mine, other), jnp.where(low, other, mine)
    rows = [jnp.concatenate([left[:, at], right[:, at]], axis=1) for at in (slice(0, half), slice(half, None))]
    whole = jnp.concatenate(rows, axis=0)
    return whole, others


def shards(queries, keys, values, out_weight, out_cotangent, offsets):
    rows_dev, feature = queries.shape[1:]
    cotangent = out_cotangent[0]
    n3 = rows_dev // 4
    far, near, mid = pick(offsets, keys, values)
    fars = [far] + [swap(far, bits) for bits in (1, 2, 3)]
    cross = swap(jnp.concatenate(fars, axis=0), 4)
    near_pair, mid2, mid3 = swap(near, 1), swap(mid, 2), swap(mid, 3)
    late_cotangent, (mid2,) = after(cotangent, [mid2])
    grads = jnp.dot(late_cotangent, out_weight, preferred_element_type=F32).astype(BF16)
    gathered = [near_pair, mid2, mid3] + fars + [cross]
    own_parts = attend_own(GROUPS[0], queries, keys, values, near, mid, far)
    results = attend_both(GROUPS[0], queries, keys, values, grads, near, mid, gathered, own_parts)
    attended, query_grad, local, own1, own2, far_grad, back = results[:7]
    cross_back = swap(back, 4)
    back1, back2, back3 = [swap(block, bits) for bits, block in zip((1, 2, 3), results[7:])]
    mixed = lax.dot_general(
        attended, out_weight, (((1,), (1,)), ((), ())), preferred_element_type=F32
    ).astype(BF16)
    share, sent = plane_share(cotangent, attended)
    share, (mixed,) = after(share, [mixed])
    far_grad, (back1, back2) = after(far_grad, [back1, back2])
    far_grad = (far_grad.astype(F32) + cross_back.astype(F32)).astype(BF16)
    far_parts = [far_grad[bits * n3 : (bits + 1) * n3] for bits in range(4)]
    rows, half = share.shape[0] // RUN, share.shape[1]
    place = lax.axis_index("seq") % RUN
    packed = rows // 2
    share_parts = []
    for bits in range(4):
        part = lax.dynamic_slice_in_dim(share, (place ^ bits) * rows, rows, 0)
        share_parts.append(jnp.concatenate([part[:packed], part[packed:]], axis=1))
    total = share_parts[0].astype(F32)
    far_back = []
    for bits in (1, 2, 3):
        padded = jnp.pad(share_parts[bits], ((0, -packed % 8), (0, feature - 2 * half)))
        arrived = swap(jnp.concatenate([far_parts[bits], padded], axis=0), bits)
        far_back.append(arrived)
        total = total + arrived[n3 : n3 + packed, : 2 * half].astype(F32)
    tiles = lax.axis_size("dp") * lax.axis_size("seq") * rows_dev
    local = local.reshape(2, rows_dev, feature)
    base = spread(
        offsets,
        (local, local),
        ((0, ((own1, 0), (back1, 0))), (1, ((own2, 0), (back1, rows_dev), (back2, 0), (back3, 0)))),
        F32,
    )
    total, base = after(total.astype(BF16), base)
    key_grad, value_grad = spread(
        offsets, base, ((2, tuple((block, 0) for block in [far_grad] + far_back)),), BF16
    )
    weight_grad, (key_grad, value_grad) = slides_total(
        total, 1.0 / math.sqrt(tiles), [key_grad, value_grad]
    )
    return mixed[None], query_grad, key_grad, value_grad, weight_grad


def solution(mesh):
    split = P("dp", "seq", None)
    return jax.shard_map(
        shards,
        mesh=mesh,
        in_specs=(split, split, split, P(), split, P()),
        out_specs=(split, split, split, split, P("seq", None)),
        check_vma=False,
    )
```
